128 devices in a mesh: panels: 128 (over x, y, z, core).
Axes of the slice: x: 4, y: 4, z: 4, core: 2. Of those that a mesh axis runs over, the one named last changes fastest.
Arguments:
- excitation: bfloat16 [64, 524288], P(None, 'panels'), may hold values from -6 to 6
- near_tiles: bfloat16 [2048, 5, 256, 256], P('panels'), may hold values from -0.15625 to 0.15625
- near_offset: int32 [2048, 5], P('panels'), may hold values from -16 to 16, as said below
- near_count: int32 [2048], P('panels'), may hold values from 1 to 5, as said below
- far_src: int32 [128, 16], replicated, may hold values from 0 to 127, as said below
- far_count: int32 [128], replicated, may hold values from 1 to 16
- source_factor: bfloat16 [16, 32, 524288], P(None, None, 'panels'), may hold values from -0.09375 to 0.09375
- target_factor: bfloat16 [16, 32, 524288], P(None, None, 'panels'), may hold values from -0.25 to 0.25
Outputs:
- krylov: float32 [5, 64, 524288], P(None, None, 'panels')
The draws below stay inside these ranges and needn't reach their ends.
Inputs may be any that keep to these rules, and one draw needn't show every extreme that they name: `near_offset`: offsets within one leaf are distinct. `near_count`: some leaf has 5 live slots. `far_src`: within a row the entries are distinct and never the row itself. Counting live slots only, every block row is the source of at most 16 far blocks, and some block row of exactly 16.
All inputs are finite; a program needn't handle non-finite values.
Results may differ from the reference program's by a relative error of at most 0.0095.
Values may be sent and summed in bfloat16 or wider, within the bound.
No kernel may reach another device: no remote copies, remote signals or barrier semaphores. Data moves between devices by JAX's collectives and lax.ppermute only.
A program may use at most 128 MiB of HBM per device.

```python
import jax
import jax.numpy as jnp
from jax import lax

LEAF = 256
EXCITE = 64
RANK = 32
NEAR = 5
FAR = 16
ITERS = 5
LEAVES_DEV = 16
PANELS_DEV = 4096
LEAVES = 2048
PANELS = 524288
DEVS = 128


def draw_near_offset(key, part):
    choices_total = 2 * LEAVES_DEV + 1
    scores = jax.random.randint(key, (LEAVES, choices_total), 0, 1 << 20) * 128
    scores = scores + jnp.arange(choices_total, dtype=jnp.int32)[None, :]
    order = jnp.argsort(scores, axis=1)
    return (order[:, :NEAR] - LEAVES_DEV).astype(jnp.int32)


def draw_near_count(key, part):
    first_key, second_key = jax.random.split(key)
    counts = jax.random.randint(first_key, (LEAVES,), 1, NEAR + 1)
    pivot = jax.random.randint(second_key, (), 0, LEAVES)
    return counts.at[pivot].set(NEAR).astype(jnp.int32)


def far_plan(key):
    base = jax.random.fold_in(key, 7)
    perm_key, offset_key, slot_key, pivot_key = jax.random.split(base, 4)
    order = jax.random.permutation(perm_key, DEVS).astype(jnp.int32)
    inverse = jnp.zeros((DEVS,), jnp.int32).at[order].set(jnp.arange(DEVS, dtype=jnp.int32))
    offset_scores = jax.random.randint(offset_key, (DEVS - 1,), 0, 1 << 16) * DEVS
    offset_scores = offset_scores + jnp.arange(DEVS - 1, dtype=jnp.int32)
    offsets = (jnp.argsort(offset_scores)[:FAR] + 1).astype(jnp.int32)
    slot_scores = jax.random.randint(slot_key, (DEVS, FAR), 0, 1 << 16) * FAR
    slot_scores = slot_scores + jnp.arange(FAR, dtype=jnp.int32)[None, :]
    slot_order = jnp.argsort(slot_scores, axis=1).astype(jnp.int32)
    shifts = jnp.take(offsets, slot_order)
    far_src = jnp.take(inverse, (order[:, None] + shifts) % DEVS)
    pivot = jax.random.randint(pivot_key, (), 0, DEVS)
    full_rows = jnp.take(inverse, (order[pivot] - offsets) % DEVS)
    return (far_src.astype(jnp.int32), full_rows.astype(jnp.int32))


def draw_far_src(key, part):
    far_src, full_rows = far_plan(key)
    return far_src


def draw_far_count(key, part):
    far_src, full_rows = far_plan(key)
    own = jax.random.fold_in(key, 11)
    first_key, second_key = jax.random.split(own)
    left = jax.random.randint(first_key, (DEVS,), 0, FAR + 1)
    right = jax.random.randint(second_key, (DEVS,), 0, FAR + 1)
    counts = jnp.clip(1 + left * right // FAR, 1, FAR)
    return counts.at[full_rows].set(FAR).astype(jnp.int32)


def level_of(own_key, dims, pieces, low, high):
    factor_of, own = 1.0, jax.random.fold_in(own_key, 6)
    for axis_at, blocks in pieces:
        heights = jnp.exp(jax.random.uniform(jax.random.fold_in(own, axis_at), (blocks,), jnp.float32, low / len(pieces), high / len(pieces)))
        factor_of = factor_of * jnp.repeat(heights, dims[axis_at] // blocks).reshape([-1 if axis == axis_at else 1 for axis in range(len(dims))])
    return factor_of


def bell_draw(rng, dims, width, bound, shards=(), kind=jnp.bfloat16):
    values = width * jax.random.normal(rng, dims, jnp.float32)
    if shards:
        values = values * level_of(rng, dims, shards, -0.22, 0.18)
    return jnp.clip(values, -bound, bound).astype(kind)


def setup_inputs(seed: int = 0) -> dict:
    splits = jax.random.split(jax.random.key(seed), 9)
    excitation = bell_draw(splits[0], (EXCITE, PANELS), 1.0, 6.0, ((1, 128),))
    near_tiles = bell_draw(splits[1], (LEAVES, NEAR, LEAF, LEAF), (NEAR * LEAF) ** -0.5, 0.15625, ((0, 128),))
    near_offset = draw_near_offset(jax.random.fold_in(splits[8], 71), 0)
    near_count = draw_near_count(jax.random.fold_in(splits[8], 71), 0)
    far_src = draw_far_src(jax.random.fold_in(splits[8], 71), 0)
    far_count = draw_far_count(jax.random.fold_in(splits[8], 71), 0)
    source_factor = bell_draw(splits[6], (FAR, RANK, PANELS), PANELS_DEV ** -0.5, 0.09375, ((2, 128),))
    target_factor = bell_draw(splits[7], (FAR, RANK, PANELS), (RANK * FAR) ** -0.5, 0.25, ((2, 128),))
    return dict(excitation=excitation, near_tiles=near_tiles, near_offset=near_offset, near_count=near_count, far_src=far_src, far_count=far_count, source_factor=source_factor, target_factor=target_factor)


def out_ranks(far_src, far_count):
    row_total, slot_count = far_src.shape
    live_far = jnp.arange(slot_count, dtype=jnp.int32)[None, :] < far_count[:, None]
    owners = jnp.arange(row_total, dtype=jnp.int32)
    hits = ((far_src.reshape(-1)[:, None] == owners[None, :]) & live_far.reshape(-1)[:, None]).astype(jnp.int32)
    earlier = jnp.cumsum(hits, axis=0) - hits
    out_rank = jnp.sum(earlier * hits, axis=1).astype(jnp.int32)
    return out_rank.reshape(row_total, slot_count), live_far


def apply_operator(field, near_tiles, near_offset, near_count, far_src, out_rank, live_far, source_factor, target_factor):
    row_total = far_src.shape[0]
    leaf_total = near_tiles.shape[0]
    near_slots = near_tiles.shape[1]
    leaf_size = near_tiles.shape[2]
    leaves_local = leaf_total // row_total
    panels_local = leaves_local * leaf_size
    excite = field.shape[0]
    highest = lax.Precision.HIGHEST

    def coefficients(device):
        first = device * panels_local
        factor = lax.dynamic_slice_in_dim(source_factor, first, panels_local, 2).astype(jnp.float32)
        charges = lax.dynamic_slice_in_dim(field, first, panels_local, 1).astype(jnp.float32)
        return jnp.einsum('jrp,mp->jrm', factor, charges, precision=highest).astype(jnp.bfloat16)

    table = lax.map(coefficients, jnp.arange(row_total, dtype=jnp.int32))
    leaves = field.reshape(excite, leaf_total, leaf_size)

    def block_row(device):
        first_leaf = device * leaves_local
        tiles = lax.dynamic_slice_in_dim(near_tiles, first_leaf, leaves_local, 0).astype(jnp.float32)
        offsets = lax.dynamic_slice_in_dim(near_offset, first_leaf, leaves_local, 0)
        counts = lax.dynamic_slice_in_dim(near_count, first_leaf, leaves_local, 0)
        source_leaf = (first_leaf + jnp.arange(leaves_local, dtype=jnp.int32)[:, None] + offsets) % leaf_total
        picked = jnp.take(leaves, source_leaf.reshape(-1).astype(jnp.int32), axis=1)
        picked = picked.reshape(excite, leaves_local, near_slots, leaf_size).astype(jnp.float32)
        live_near = jnp.arange(near_slots, dtype=jnp.int32)[None, :] < counts[:, None]
        picked = jnp.where(live_near[None, :, :, None], picked, jnp.zeros_like(picked))
        near_part = jnp.einsum('ijab,mijb->mia', tiles, picked, precision=highest).reshape(excite, panels_local)
        sources = far_src[device]
        ranks = out_rank[device]
        live_slot = live_far[device]
        coef = table[sources, ranks].astype(jnp.float32)
        coef = jnp.where(live_slot[:, None, None], coef, jnp.zeros_like(coef))
        factor = lax.dynamic_slice_in_dim(target_factor, device * panels_local, panels_local, 2).astype(jnp.float32)
        far_part = jnp.einsum('jrm,jrp->mp', coef, factor, precision=highest)
        return near_part + far_part

    rows_out = lax.map(block_row, jnp.arange(row_total, dtype=jnp.int32))
    return jnp.transpose(rows_out, (1, 0, 2)).reshape(excite, row_total * panels_local)


def reference(excitation, near_tiles, near_offset, near_count, far_src, far_count, source_factor, target_factor):
    out_rank, live_far = out_ranks(far_src, far_count)
    current = excitation
    results = []
    for step in range(ITERS):
        result = apply_operator(current, near_tiles, near_offset, near_count, far_src, out_rank, live_far, source_factor, target_factor)
        results.append(result)
        current = result.astype(jnp.bfloat16)
    return jnp.stack(results, axis=0)
```

```python
import jax
import jax.numpy as jnp
from jax import lax
from jax.experimental import pallas as pl
from jax.experimental.pallas import tpu as pltpu
from jax.sharding import PartitionSpec as P

ITERS = 5
BATCH = 8
F32 = jnp.float32
BF16 = jnp.bfloat16
NT = (((1,), (1,)), ((), ()))
VMEM = pl.BlockSpec(memory_space=pltpu.VMEM)
SMEM = pl.BlockSpec(memory_space=pltpu.SMEM)
ANY = pl.BlockSpec(memory_space=pl.ANY)
LIMIT = 12 * 2**20


def nt(a, b):
    return lax.dot_general(a, b, NT, preferred_element_type=F32)


def pinned(x):
    return pltpu.with_memory_space_constraint(x, pltpu.VMEM)


def params():
    return pltpu.CompilerParams(vmem_limit_bytes=LIMIT)


def cost(flops, touched):
    return pl.CostEstimate(flops=flops, bytes_accessed=touched, transcendentals=0)


def place(dest, x, send):
    slots = x.shape[0] // 16
    for q in range(slots):

        @pl.when(dest[q] >= 0)
        def _():
            send[dest[q]] = x[16 * q : 16 * q + 16]


def project(source, leaf):
    leaves = source.shape[2] // 256
    halves = []
    for h in range(2):
        acc = nt(source[h, :, :256], leaf(0))
        for i in range(1, leaves):
            acc += nt(source[h, :, 256 * i : 256 * i + 256], leaf(i))
        halves.append(acc)
    return jnp.concatenate(halves, axis=1).astype(BF16)


def first_kernel(dest, field, factor, source, leaves, send, sems):
    slots = factor.shape[0]
    parts = 8
    width = field.shape[1] // parts
    copies = []
    for c in range(parts):
        cols = pl.ds(c * width, width)
        for h in range(2):
            for q in range(slots):
                copies.append(
                    pltpu.make_async_copy(
                        factor.at[q, pl.ds(16 * h, 16), cols],
                        source.at[h, pl.ds(16 * q, 16), cols],
                        sems.at[c],
                    )
                )
    for copy in copies:
        copy.start()
    for i in range(leaves.shape[0]):
        leaves[i] = field[:, 256 * i : 256 * i + 256]
    accs = [None, None]
    per = 2 * slots
    for c in range(parts):
        for copy in copies[c * per : (c + 1) * per]:
            copy.wait()
        for h in range(2):
            for b in range(width // 256):
                i = c * (width // 256) + b
                term = nt(source[h, :, 256 * i : 256 * i + 256], leaves[i])
                accs[h] = term if accs[h] is None else accs[h] + term
    place(dest, jnp.concatenate(accs, axis=1).astype(BF16), send)


def run_list(lists, counts, which, tiles, field, acc):
    groups = counts[which]

    def body(g, carry):
        found = []
        for b in range(BATCH):
            e = g * BATCH + b
            found.append(nt(field[lists[which, 1, e]], tiles[lists[which, 0, e]]))
        for b in range(BATCH):
            e = g * BATCH + b
            acc[lists[which, 2, e]] += found[b]
        return carry

    lax.fori_loop(0, groups, body, 0)


def setup_kernel(offset, count, field, near, factor, tiles, target, acc, lists, counts, out, sem, tsem):
    leaves, slots = offset.shape[0], near.shape[1]
    blocks = factor.shape[0]

    def fetch(e):
        return pltpu.make_async_copy(near.at[e // slots, e % slots], tiles.at[e], sem)

    moved = [
        pltpu.make_async_copy(
            factor.at[k, pl.ds(16 * h, 16)], target.at[pl.ds(256 * h + 16 * k, 16)], tsem
        )
        for h in range(2)
        for k in range(blocks)
    ]

    def leaf_body(i, filled):
        def slot_body(j, filled):
            fetch(i * slots + j).start()
            place_at = i + offset[i, j]
            which = jnp.where(place_at < 0, 1, jnp.where(place_at >= leaves, 2, 0))
            at = jnp.where(which == 0, filled[0], jnp.where(which == 1, filled[1], filled[2]))
            lists[which, 0, at] = i * slots + j
            lists[which, 1, at] = jnp.where(
                place_at < 0, place_at + leaves, jnp.where(place_at >= leaves, place_at - leaves, place_at)
            )
            lists[which, 2, at] = i
            return tuple(filled[w] + jnp.where(which == w, 1, 0) for w in range(3))

        return lax.fori_loop(0, count[i], slot_body, filled)

    zero = jnp.int32(0)
    filled = lax.fori_loop(0, leaves, leaf_body, (zero, zero, zero))
    for copy in moved:
        copy.start()
    for w in range(3):
        groups = (filled[w] + BATCH - 1) // BATCH

        def fill(e, carry, w=w):
            lists[w, 0, e] = 0
            lists[w, 1, e] = 0
            lists[w, 2, e] = leaves
            return carry

        lax.fori_loop(filled[w], groups * BATCH, fill, 0)
        counts[w] = groups
    acc[...] = jnp.zeros_like(acc)

    def wait_leaf(i, carry):
        def wait_slot(j, carry):
            fetch(i * slots + j).wait()
            return carry

        return lax.fori_loop(0, count[i], wait_slot, carry)

    lax.fori_loop(0, leaves, wait_leaf, 0)
    run_list(lists, counts, 0, tiles, field, acc)
    for copy in moved:
        copy.wait()


def local_kernel(step, lists, counts, tiles, field, done, _, acc, out, sem):
    copy = pltpu.make_async_copy(done, out.at[step - 1], sem)
    copy.start()
    acc[...] = jnp.zeros_like(acc)
    run_list(lists, counts, 0, tiles, field, acc)
    copy.wait()


def far_kernel(src, received, target, _, acc, picked):
    slots = picked.shape[0] // 16
    for k in range(slots):

        @pl.when(src[k] >= 0)
        def _():
            picked[16 * k : 16 * k + 16] = received[src[k]]

        @pl.when(src[k] < 0)
        def _():
            picked[16 * k : 16 * k + 16] = jnp.zeros((16, 128), BF16)

    turned = picked[...].astype(F32).T.astype(BF16)
    coef = jnp.concatenate([turned[:64], turned[64:]], axis=1)
    for i in range(target.shape[1] // 256):
        acc[i] += jnp.dot(coef, target[:, 256 * i : 256 * i + 256], preferred_element_type=F32)


def finish_kernel(lists, counts, dest, tiles, left, right, source, acc_in, acc, done, field, send):
    run_list(lists, counts, 1, tiles, left, acc)
    run_list(lists, counts, 2, tiles, right, acc)
    for i in range(field.shape[0]):
        value = acc[i]
        done[:, 256 * i : 256 * i + 256] = value
        field[i] = value.astype(BF16)
    place(dest, project(source, lambda i: field[i]), send)


def last_kernel(step, lists, counts, tiles, left, right, acc_in, out_in, acc, out, done, sems):
    run_list(lists, counts, 1, tiles, left, acc)
    run_list(lists, counts, 2, tiles, right, acc)
    copies = []
    for i in range(done.shape[1] // 256):
        cols = pl.ds(256 * i, 256)
        done[:, 256 * i : 256 * i + 256] = acc[i]
        copies.append(pltpu.make_async_copy(done.at[:, cols], out.at[step, :, cols], sems.at[i]))
        copies[-1].start()
    for copy in copies:
        copy.wait()


def far_lists(far_src, far_count, own):
    rows, slots = far_src.shape
    live = jnp.arange(slots, dtype=jnp.int32)[None, :] < far_count[:, None]
    has = jnp.any((far_src == own) & live, axis=1)
    order = jnp.arange(rows, dtype=jnp.int32)
    rank = jnp.sum((has[None, :] & (order[None, :] < order[:, None])).astype(jnp.int32), axis=1)
    hit = has[None, :] & (rank[None, :] == jnp.arange(slots, dtype=jnp.int32)[:, None])
    dest = jnp.max(jnp.where(hit, order[None, :], -1), axis=1)
    own_src = lax.dynamic_index_in_dim(far_src, own, 0, keepdims=False)
    own_count = lax.dynamic_index_in_dim(far_count, own, 0, keepdims=False)
    src = jnp.where(jnp.arange(slots, dtype=jnp.int32) < own_count, own_src, -1)
    return dest, src


def shards(
    excitation, near_tiles, near_offset, near_count, far_src, far_count, source_factor, target_factor
):
    excite, panels = excitation.shape
    leaves, near_slots, leaf = near_tiles.shape[:3]
    rows, slots = far_src.shape
    rank = source_factor.shape[1]
    count = lax.axis_size("panels")
    dest, src = far_lists(far_src, far_count, lax.axis_index("panels"))

    tile_total = leaves * near_slots
    entries = tile_total + BATCH
    send_type = pltpu.VMEM((rows, rank // 2, 2 * excite), BF16)
    field_type = pltpu.VMEM((leaves, excite, leaf), BF16)
    acc_type = pltpu.VMEM((leaves + 1, excite, leaf), F32)
    out_type = jax.ShapeDtypeStruct((ITERS, excite, panels), F32)
    done_type = pltpu.VMEM((excite, panels), F32)

    source, field, send = pl.pallas_call(
        first_kernel,
        out_shape=(pltpu.VMEM((2, slots * rank // 2, panels), BF16), field_type, send_type),
        in_specs=[SMEM, VMEM, ANY],
        out_specs=(VMEM, VMEM, VMEM),
        scratch_shapes=[pltpu.SemaphoreType.DMA((8,))],
        compiler_params=params(),
        cost_estimate=cost(2 * slots * rank * panels * excite, 2 * slots * rank * panels),
        name="first",
    )(dest, excitation, source_factor)

    right_of = [(i, (i + 1) % count) for i in range(count)]
    left_of = [((i + 1) % count, i) for i in range(count)]
    out = done = tiles = target = lists = counts = None
    for step in range(ITERS):
        received = lax.all_to_all(send, "panels", split_axis=0, concat_axis=0, tiled=True)
        left = lax.ppermute(field, "panels", right_of)
        right = lax.ppermute(field, "panels", left_of)
        if step == 0:
            tiles, target, acc, lists, counts, out = pl.pallas_call(
                setup_kernel,
                out_shape=(
                    pltpu.VMEM((tile_total, leaf, leaf), BF16),
                    pltpu.VMEM((slots * rank, panels), BF16),
                    acc_type,
                    jax.ShapeDtypeStruct((3, 3, entries), jnp.int32),
                    jax.ShapeDtypeStruct((3,), jnp.int32),
                    out_type,
                ),
                in_specs=[SMEM, SMEM, VMEM, ANY, ANY],
                out_specs=(VMEM, VMEM, VMEM, SMEM, SMEM, ANY),
                scratch_shapes=[pltpu.SemaphoreType.DMA, pltpu.SemaphoreType.DMA],
                compiler_params=params(),
                cost_estimate=cost(tile_total * 2**22, 2 * tile_total * leaf * leaf),
                name="setup",
            )(near_offset, near_count, pinned(field), near_tiles, target_factor)
        else:
            acc, out = pl.pallas_call(
                lambda *refs, step=step: local_kernel(step, *refs),
                out_shape=(acc_type, out_type),
                in_specs=[SMEM, SMEM, VMEM, VMEM, VMEM, ANY],
                out_specs=(VMEM, ANY),
                input_output_aliases={5: 1},
                scratch_shapes=[pltpu.SemaphoreType.DMA],
                compiler_params=params(),
                cost_estimate=cost(tile_total * 2**22, 2**22),
                name="local",
            )(lists, counts, pinned(tiles), pinned(field), pinned(done), out)
        acc = pl.pallas_call(
            far_kernel,
            out_shape=acc_type,
            in_specs=[SMEM, VMEM, VMEM, VMEM],
            out_specs=VMEM,
            input_output_aliases={3: 0},
            scratch_shapes=[pltpu.VMEM((slots * rank // 2, 2 * excite), BF16)],
            compiler_params=params(),
            cost_estimate=cost(2 * slots * rank * panels * excite, 2**22),
            name="far",
        )(src, pinned(received), pinned(target), pinned(acc))
        if step < ITERS - 1:
            acc, done, field, send = pl.pallas_call(
                finish_kernel,
                out_shape=(acc_type, done_type, field_type, send_type),
                in_specs=[SMEM, SMEM, SMEM, VMEM, VMEM, VMEM, VMEM, VMEM],
                out_specs=(VMEM, VMEM, VMEM, VMEM),
                input_output_aliases={7: 0},
                compiler_params=params(),
                cost_estimate=cost(tile_total * 2**22, 2**22),
                name="finish",
            )(lists, counts, dest, pinned(tiles), pinned(left), pinned(right), pinned(source), pinned(acc))
        else:
            acc, out = pl.pallas_call(
                lambda *refs, step=step: last_kernel(step, *refs),
                out_shape=(acc_type, out_type),
                in_specs=[SMEM, SMEM, VMEM, VMEM, VMEM, VMEM, ANY],
                out_specs=(VMEM, ANY),
                input_output_aliases={5: 0, 6: 1},
                scratch_shapes=[pltpu.VMEM((excite, panels), F32), pltpu.SemaphoreType.DMA((leaves,))],
                compiler_params=params(),
                cost_estimate=cost(tile_total * 2**22, 2**22),
                name="last",
            )(lists, counts, pinned(tiles), pinned(left), pinned(right), pinned(acc), out)
    return out


def solution(mesh):
    in_specs = (
        P(None, "panels"),
        P("panels", None, None, None),
        P("panels", None),
        P("panels"),
        P(),
        P(),
        P(None, None, "panels"),
        P(None, None, "panels"),
    )
    out_specs = P(None, None, "panels")
    return jax.shard_map(shards, mesh=mesh, in_specs=in_specs, out_specs=out_specs, check_vma=False)
```

```python
import jax
import jax.numpy as jnp
from jax import lax
from jax.experimental import pallas as pl
from jax.experimental.pallas import tpu as pltpu
from jax.sharding import PartitionSpec as P

ITERS = 5
BATCH = 8
PARTS = 4
F32 = jnp.float32
BF16 = jnp.bfloat16
NT = (((1,), (1,)), ((), ()))
VMEM = pl.BlockSpec(memory_space=pltpu.VMEM)
SMEM = pl.BlockSpec(memory_space=pltpu.SMEM)
ANY = pl.BlockSpec(memory_space=pl.ANY)
LIMIT = 24 * 2**20


def nt(a, b):
    return lax.dot_general(a, b, NT, preferred_element_type=F32)


def pinned(x):
    return pltpu.with_memory_space_constraint(x, pltpu.VMEM)


def streamed(x):
    return pltpu.with_memory_space_constraint(x, pltpu.HBM)


def params():
    return pltpu.CompilerParams(vmem_limit_bytes=LIMIT)


def cost(flops, touched):
    return pl.CostEstimate(flops=flops, bytes_accessed=touched, transcendentals=0)


def place(dest, x, send, sem):
    slots = x.shape[0] // 16

    def copy(q):
        return pltpu.make_async_copy(x.at[pl.ds(16 * q, 16)], send.at[dest[q]], sem.at[q])

    for act in ("start", "wait"):
        for q in range(slots):

            @pl.when(dest[q] >= 0)
            def _():
                getattr(copy(q), act)()

        if act == "start":
            yield
    yield


def project(source, accs, i, leaf):
    out = []
    for h in range(2):
        part = source[h, :, :, 256 * i : 256 * i + 256]
        term = nt(part.reshape(-1, 256), leaf)
        out.append(term if accs is None else accs[h] + term)
    return out


def half_copy(factor, wide, sems, c, h):
    width = wide.shape[3] // sems.shape[0]
    cols = pl.ds(c * width, width)
    return pltpu.make_async_copy(factor.at[:, pl.ds(16 * h, 16), cols], wide.at[h, :, :, cols], sems.at[c, h])


def start_halves(factor, wide, sems):
    for c in range(sems.shape[0]):
        for h in range(2):
            half_copy(factor, wide, sems, c, h).start()


def wait_halves(factor, wide, sems, c):
    for h in range(2):
        half_copy(factor, wide, sems, c, h).wait()


def first_kernel(dest, field_in, factor, send, field, source, x, sems, psem, fsem):
    brought = pltpu.make_async_copy(field_in, field, fsem)
    brought.start()
    start_halves(factor, source, sems)
    brought.wait()
    parts = sems.shape[0]
    per = field.shape[1] // 256 // parts
    accs = None
    for c in range(parts):
        wait_halves(factor, source, sems, c)
        for i in range(c * per, c * per + per):
            accs = project(source, accs, i, field[:, 256 * i : 256 * i + 256])
    x[...] = jnp.concatenate(accs, axis=1).astype(BF16)
    for _ in place(dest, x, send, psem):
        pass


def fetch_list(lists, groups, which, base, near, tiles, sem_of):
    def body(g, carry):
        for b in range(BATCH):
            e = g * BATCH + b
            pltpu.make_async_copy(near.at[lists[which, 0, e]], tiles.at[base + e], sem_of(g)).start()
        return carry

    lax.fori_loop(0, groups, body, 0)


def arrived(near, tiles, sem, at):
    pltpu.make_async_copy(near.at[pl.ds(0, BATCH)], tiles.at[pl.ds(at, BATCH)], sem).wait()


def run_list(lists, groups, which, base, tiles, field, acc, ready=None):
    def body(g, carry):
        if ready is not None:
            ready(g)
        found = []
        for b in range(BATCH):
            e = g * BATCH + b
            at = pl.multiple_of(lists[which, 1, e], 256)
            found.append(nt(field[:, pl.ds(at, 256)], tiles[base + e]))
        for b in range(BATCH):
            e = g * BATCH + b
            acc[lists[which, 2, e]] += found[b]
        return carry

    lax.fori_loop(0, groups, body, 0)


def own_part(lists, counts, field, near, acc, others, tiles, sems, osem, also=None):
    fetch_list(lists, counts[0], 0, 0, near, tiles, lambda g: sems.at[g])
    fetch_list(lists, counts[1], 1, 0, near, others, lambda g: osem)
    fetch_list(lists, counts[2], 2, counts[1] * BATCH, near, others, lambda g: osem)
    if also is not None:
        also.start()
    acc[...] = jnp.zeros_like(acc)
    run_list(
        lists, counts[0], 0, 0, tiles, field, acc, lambda g: arrived(near, tiles, sems.at[g], g * BATCH)
    )

    def body(g, carry):
        arrived(near, others, osem, g * BATCH)
        return carry

    lax.fori_loop(0, counts[1] + counts[2], body, 0)


def setup_kernel(
    offset, count, field, near, source_factor, target_factor,
    acc, others, source, target, lists, counts, out, tiles, sems, osem, ssems, tsems,
):
    leaves = count.shape[0]
    slots = near.shape[0] // leaves

    def leaf_body(i, filled):
        def slot_body(j, filled):
            at_leaf = i + offset[j, i]
            which = jnp.where(at_leaf < 0, 1, jnp.where(at_leaf >= leaves, 2, 0))
            at = jnp.where(which == 0, filled[0], jnp.where(which == 1, filled[1], filled[2]))
            lists[which, 0, at] = i * slots + j
            lists[which, 1, at] = 256 * jnp.where(
                which == 1, at_leaf + leaves, jnp.where(which == 2, at_leaf - leaves, at_leaf)
            )
            lists[which, 2, at] = i
            return tuple(filled[w] + jnp.where(which == w, 1, 0) for w in range(3))

        return lax.fori_loop(0, count[i], slot_body, filled)

    zero = jnp.int32(0)
    filled = lax.fori_loop(0, leaves, leaf_body, (zero, zero, zero))
    for w in range(3):
        groups = (filled[w] + BATCH - 1) // BATCH

        def fill(e, carry, w=w):
            lists[w, 0, e] = 0
            lists[w, 1, e] = 0
            lists[w, 2, e] = leaves
            return carry

        lax.fori_loop(filled[w], groups * BATCH, fill, 0)
        counts[w] = groups
    start_halves(source_factor, source, ssems)
    start_halves(target_factor, target, tsems)
    own_part(lists, counts, field, near, acc, others, tiles, sems, osem)
    for c in range(ssems.shape[0]):
        wait_halves(source_factor, source, ssems, c)
        wait_halves(target_factor, target, tsems, c)


def local_kernel(step, lists, counts, field, near, done, _, acc, others, out, tiles, sems, osem, dsem):
    copy = pltpu.make_async_copy(done, out.at[step - 1], dsem)
    own_part(lists, counts, field, near, acc, others, tiles, sems, osem, copy)
    copy.wait()


def others_part(lists, counts, tiles, left, right, acc):
    run_list(lists, counts[1], 1, 0, tiles, left, acc)
    run_list(lists, counts[2], 2, counts[1] * BATCH, tiles, right, acc)


def first_others_kernel(lists, counts, tiles, left, right, source, _, acc, x):
    others_part(lists, counts, tiles, left, right, acc)
    accs = None
    for i in range(acc.shape[0] - 1):
        accs = project(source, accs, i, acc[i].astype(BF16))
    x[...] = jnp.concatenate(accs, axis=1)


def others_kernel(lists, counts, tiles, left, right, factor, _, acc, x, source, sems):
    start_halves(factor, source, sems)
    others_part(lists, counts, tiles, left, right, acc)
    parts = sems.shape[0]
    per = (acc.shape[0] - 1) // parts
    accs = None
    for c in range(parts):
        wait_halves(factor, source, sems, c)
        for i in range(c * per, c * per + per):
            accs = project(source, accs, i, acc[i].astype(BF16))
    x[...] = jnp.concatenate(accs, axis=1)


def last_others_kernel(lists, counts, tiles, left, right, _, acc):
    others_part(lists, counts, tiles, left, right, acc)


def gram_kernel(source, target, gram):
    panels = source.shape[3]
    for h in range(2):
        for g in range(2):
            gram[h, g] = nt(source[h].reshape(-1, panels), target[g].reshape(-1, panels)).astype(BF16)


def pick(far_src, far_count, received, picked):
    own = lax.axis_index("panels")
    live = far_count[own]
    for k in range(picked.shape[0] // 16):
        block = received[far_src[k, own]]
        picked[16 * k : 16 * k + 16] = jnp.where(k < live, block, jnp.zeros_like(block))


def expand(target_factor, acc, picked, wide, tsems, use, passed):
    turned = picked[...].astype(F32).T.astype(BF16)
    excite = turned.shape[0] // 2
    parts = tsems.shape[0]
    per = wide.shape[3] // 256 // parts
    for c in range(parts):
        wait_halves(target_factor, wide, tsems, c)
        for i in range(c * per, c * per + per):
            cols = slice(256 * i, 256 * i + 256)
            value = acc[i]
            for h in range(2):
                value += jnp.dot(
                    turned[excite * h : excite * h + excite],
                    wide[h, :, :, cols].reshape(-1, 256),
                    preferred_element_type=F32,
                )
            use(cols, value)
        passed(c)


def far_kernel(
    far_src, far_count, dest, received, target_factor, gram_in, acc, x, field, send, done,
    gram, picked, ready, wide, tsems, psems, gsem,
):
    brought = pltpu.make_async_copy(gram_in, gram, gsem)
    brought.start()
    start_halves(target_factor, wide, tsems)
    pick(far_src, far_count, received, picked)
    excite = picked.shape[1] // 2
    brought.wait()
    parts = []
    for h in range(2):
        part = x[:, excite * h : excite * h + excite]
        for g in range(2):
            part += jnp.dot(
                gram[h, g], picked[:, excite * g : excite * g + excite], preferred_element_type=F32
            )
        parts.append(part)
    ready[...] = jnp.concatenate(parts, axis=1).astype(BF16)
    placed = place(dest, ready, send, psems)
    next(placed)

    def use(cols, value):
        done[:, cols] = value
        field[:, cols] = value.astype(BF16)

    expand(target_factor, acc, picked, wide, tsems, use, lambda c: None)
    next(placed)


def last_kernel(step, far_src, far_count, received, target_factor, acc, _, out, picked, wide, done, tsems, osems):
    start_halves(target_factor, wide, tsems)
    pick(far_src, far_count, received, picked)
    copies = []

    def use(cols, value):
        done[:, cols] = value

    def passed(c):
        width = done.shape[1] // osems.shape[0]
        cols = pl.ds(width * c, width)
        copies.append(pltpu.make_async_copy(done.at[:, cols], out.at[step, :, cols], osems.at[c]))
        copies[-1].start()

    expand(target_factor, acc, picked, wide, tsems, use, passed)
    for copy in copies:
        copy.wait()


def far_lists(far_src, far_count, own):
    rows, slots = far_src.shape
    live = jnp.arange(slots, dtype=jnp.int32)[None, :] < far_count[:, None]
    has = jnp.any((far_src == own) & live, axis=1)
    order = jnp.arange(rows, dtype=jnp.int32)
    rank = jnp.sum((has[None, :] & (order[None, :] < order[:, None])).astype(jnp.int32), axis=1)
    hit = has[None, :] & (rank[None, :] == jnp.arange(slots, dtype=jnp.int32)[:, None])
    dest = jnp.max(jnp.where(hit, order[None, :], -1), axis=1)
    return dest


def shards(
    excitation, near_tiles, near_offset, near_count, far_src, far_count, source_factor, target_factor
):
    excite, panels = excitation.shape
    leaves, near_slots, leaf = near_tiles.shape[:3]
    rows, slots = far_src.shape
    rank = source_factor.shape[1]
    count = lax.axis_size("panels")
    dest = far_lists(far_src, far_count, lax.axis_index("panels"))

    tile_total = leaves * near_slots
    near = streamed(near_tiles.reshape(tile_total, leaf, leaf))
    source_factor, target_factor = streamed(source_factor), streamed(target_factor)
    entries = tile_total + BATCH
    half = slots * rank // 2
    send_type = pltpu.HBM((rows, rank // 2, 2 * excite), BF16)
    field_type = jax.ShapeDtypeStruct((excite, panels), BF16)
    acc_type = pltpu.VMEM((leaves + 1, excite, leaf), F32)
    out_type = pltpu.HBM((ITERS, excite, panels), F32)
    tiles_type = pltpu.VMEM((entries, leaf, leaf), BF16)
    half_type = pltpu.VMEM((2, slots, rank // 2, panels), BF16)
    done_type = pltpu.VMEM((excite, panels), F32)
    picked_type = pltpu.VMEM((half, 2 * excite), BF16)
    x_type = pltpu.VMEM((half, 2 * excite), F32)
    gram_shape = (2, 2, half, half)
    dma = pltpu.SemaphoreType.DMA
    groups = entries // BATCH
    far_flops = 2 * slots * rank * panels * excite

    def call(kernel, out_shape, in_specs, out_specs, scratch, flops, name, aliases=None):
        return pl.pallas_call(
            kernel,
            out_shape=out_shape,
            in_specs=in_specs,
            out_specs=out_specs,
            scratch_shapes=scratch,
            input_output_aliases=aliases or {},
            compiler_params=params(),
            cost_estimate=cost(flops, 2**22),
            name=name,
        )

    right_of = [(i, (i + 1) % count) for i in range(count)]
    left_of = [((i + 1) % count, i) for i in range(count)]
    field = send = lists = counts = out = gram = done = None
    turned_src = far_src.T
    for step in range(ITERS):
        if step == 0:
            send, field = call(
                first_kernel, (send_type, field_type), [SMEM, ANY, ANY], (ANY, VMEM),
                [half_type, picked_type, dma((PARTS, 2)), dma((slots,)), dma], far_flops, "first",
            )(dest, streamed(excitation), source_factor)
        left = lax.ppermute(field, "panels", right_of)
        right = lax.ppermute(field, "panels", left_of)
        received = lax.all_to_all(send, "panels", split_axis=0, concat_axis=0, tiled=True)
        own_scratch = [tiles_type, dma((groups,)), dma]
        if step == 0:
            acc, tiles, source, target, lists, counts, out = call(
                setup_kernel,
                (
                    acc_type, tiles_type, half_type, half_type,
                    jax.ShapeDtypeStruct((3, 3, entries), jnp.int32),
                    jax.ShapeDtypeStruct((3,), jnp.int32),
                    out_type,
                ),
                [SMEM, SMEM, VMEM, ANY, ANY, ANY], (VMEM, VMEM, VMEM, VMEM, SMEM, SMEM, ANY),
                [*own_scratch, dma((PARTS, 2)), dma((PARTS, 2))],
                tile_total * 2**22, "setup",
            )(near_offset.T, near_count, field, near, source_factor, target_factor)
            gram = call(
                gram_kernel, pltpu.HBM(gram_shape, BF16), [VMEM, VMEM], VMEM,
                [], 4 * half * half * panels * 2, "gram",
            )(pinned(source), pinned(target))
        else:
            acc, tiles, out = call(
                lambda *refs, step=step: local_kernel(step, *refs), (acc_type, tiles_type, out_type),
                [SMEM, SMEM, VMEM, ANY, VMEM, ANY], (VMEM, VMEM, ANY), [*own_scratch, dma],
                tile_total * 2**22, "local", {5: 2},
            )(lists, counts, field, near, pinned(done), streamed(out))
        near_operands = (lists, counts, pinned(tiles), left, right)
        if step == ITERS - 1:
            acc = call(
                last_others_kernel, acc_type, [SMEM, SMEM, VMEM, VMEM, VMEM, VMEM], VMEM,
                [], tile_total * 2**22, "others", {5: 0},
            )(*near_operands, pinned(acc))
            return call(
                lambda *refs, step=step: last_kernel(step, *refs),
                out_type, [SMEM, SMEM, VMEM, ANY, VMEM, ANY], ANY,
                [picked_type, half_type, done_type, dma((PARTS, 2)), dma((PARTS,))],
                far_flops, "last", {5: 0},
            )(turned_src, far_count, received, target_factor, pinned(acc), streamed(out))
        if step == 0:
            acc, x = call(
                first_others_kernel, (acc_type, x_type), [SMEM, SMEM, VMEM, VMEM, VMEM, VMEM, VMEM], (VMEM, VMEM),
                [], tile_total * 2**22, "others", {6: 0},
            )(*near_operands, pinned(source), pinned(acc))
        else:
            acc, x = call(
                others_kernel, (acc_type, x_type), [SMEM, SMEM, VMEM, VMEM, VMEM, ANY, VMEM], (VMEM, VMEM),
                [half_type, dma((PARTS, 2))], tile_total * 2**22, "others", {6: 0},
            )(*near_operands, source_factor, pinned(acc))
        field, send, done = call(
            far_kernel, (field_type, send_type, done_type),
            [SMEM, SMEM, SMEM, VMEM, ANY, ANY, VMEM, VMEM], (VMEM, ANY, VMEM),
            [
                pltpu.VMEM(gram_shape, BF16), picked_type, picked_type, half_type,
                dma((PARTS, 2)), dma((slots,)), dma,
            ],
            far_flops, "far",
        )(turned_src, far_count, dest, received, target_factor, streamed(gram), pinned(acc), pinned(x))


def solution(mesh):
    in_specs = (
        P(None, "panels"),
        P("panels", None, None, None),
        P("panels", None),
        P("panels"),
        P(),
        P(),
        P(None, None, "panels"),
        P(None, None, "panels"),
    )
    out_specs = P(None, None, "panels")
    return jax.shard_map(shards, mesh=mesh, in_specs=in_specs, out_specs=out_specs, check_vma=False)
```

```python
import jax
import jax.numpy as jnp
from jax import lax
from jax.experimental import pallas as pl
from jax.experimental.pallas import tpu as pltpu
from jax.sharding import PartitionSpec as P

ITERS = 5
BATCH = 8
PARTS = 4
F32 = jnp.float32
BF16 = jnp.bfloat16
NT = (((1,), (1,)), ((), ()))
VMEM = pl.BlockSpec(memory_space=pltpu.VMEM)
SMEM = pl.BlockSpec(memory_space=pltpu.SMEM)
ANY = pl.BlockSpec(memory_space=pl.ANY)
LIMIT = 24 * 2**20


def nt(a, b):
    return lax.dot_general(a, b, NT, preferred_element_type=F32)


def pinned(x):
    return pltpu.with_memory_space_constraint(x, pltpu.VMEM)


def streamed(x):
    return pltpu.with_memory_space_constraint(x, pltpu.HBM)


def params():
    return pltpu.CompilerParams(vmem_limit_bytes=LIMIT)


def cost(flops, touched):
    return pl.CostEstimate(flops=flops, bytes_accessed=touched, transcendentals=0)


def place(dest, x, send, sem):
    slots = x.shape[0] // 16

    def copy(q):
        return pltpu.make_async_copy(x.at[pl.ds(16 * q, 16)], send.at[dest[q]], sem.at[q])

    for act in ("start", "wait"):
        for q in range(slots):

            @pl.when(dest[q] >= 0)
            def _():
                getattr(copy(q), act)()

        if act == "start":
            yield
    yield


def project(source, accs, i, leaf):
    out = []
    for h in range(2):
        part = source[h, :, :, 256 * i : 256 * i + 256]
        term = nt(part.reshape(-1, 256), leaf)
        out.append(term if accs is None else accs[h] + term)
    return out


def half_copy(factor, wide, sems, c, h):
    width = wide.shape[3] // sems.shape[0]
    cols = pl.ds(c * width, width)
    return pltpu.make_async_copy(factor.at[:, pl.ds(16 * h, 16), cols], wide.at[h, :, :, cols], sems.at[c, h])


def start_halves(factor, wide, sems):
    for c in range(sems.shape[0]):
        for h in range(2):
            half_copy(factor, wide, sems, c, h).start()


def wait_halves(factor, wide, sems, c):
    for h in range(2):
        half_copy(factor, wide, sems, c, h).wait()


def first_kernel(dest, field_in, factor, send, field, source, x, sems, psem, fsem):
    brought = pltpu.make_async_copy(field_in, field, fsem)
    brought.start()
    start_halves(factor, source, sems)
    brought.wait()
    parts = sems.shape[0]
    per = field.shape[1] // 256 // parts
    accs = None
    for c in range(parts):
        wait_halves(factor, source, sems, c)
        for i in range(c * per, c * per + per):
            accs = project(source, accs, i, field[:, 256 * i : 256 * i + 256])
    x[...] = jnp.concatenate(accs, axis=1).astype(BF16)
    for _ in place(dest, x, send, psem):
        pass


def fetch_list(lists, groups, which, base, near, tiles, sem_of):
    def body(g, carry):
        for b in range(BATCH):
            e = g * BATCH + b
            pltpu.make_async_copy(near.at[lists[which, 0, e]], tiles.at[base + e], sem_of(g)).start()
        return carry

    lax.fori_loop(0, groups, body, 0)


def arrived(near, tiles, sem, at):
    pltpu.make_async_copy(near.at[pl.ds(0, BATCH)], tiles.at[pl.ds(at, BATCH)], sem).wait()


def run_list(lists, groups, which, base, tiles, field, acc, ready=None):
    def body(g, carry):
        if ready is not None:
            ready(g)
        found = []
        for b in range(BATCH):
            e = g * BATCH + b
            at = pl.multiple_of(lists[which, 1, e], 256)
            found.append(nt(field[:, pl.ds(at, 256)], tiles[base + e]))
        for b in range(BATCH):
            e = g * BATCH + b
            acc[lists[which, 2, e]] += found[b]
        return carry

    lax.fori_loop(0, groups, body, 0)


def own_part(lists, counts, field, mate, near, acc, others, tiles, sems, osem, both, bsems, between=None):
    panels = field.shape[1]
    brought = [
        pltpu.make_async_copy(part, both.at[:, pl.ds(panels * k, panels)], bsems.at[k])
        for k, part in enumerate((field, mate))
    ]
    for copy in brought:
        copy.start()
    fetch_list(lists, counts[0], 0, 0, near, tiles, lambda g: sems.at[g])
    fetch_list(lists, counts[1], 1, 0, near, others, lambda g: osem)
    if between is not None:
        between()
    acc[...] = jnp.zeros_like(acc)
    for copy in brought:
        copy.wait()

    def ready(g):
        arrived(near, tiles, sems.at[g], g * BATCH)

    run_list(lists, counts[0], 0, 0, tiles, both, acc, ready)

    def body(g, carry):
        arrived(near, others, osem, g * BATCH)
        return carry

    lax.fori_loop(0, counts[1], body, 0)


def setup_kernel(
    offset, count, field, mate, near, source_factor, target_factor,
    acc, others, source, gram, lists, counts, out, tiles, sems, osem, mate_here, msem, target, ssems, tsems,
):
    start_halves(source_factor, source, ssems)
    start_halves(target_factor, target, tsems)
    leaves = count.shape[0]
    slots = near.shape[0] // leaves
    odd = lax.axis_index("panels") % 2

    def leaf_body(i, filled):
        def slot_body(j, filled):
            at_leaf = i + offset[j, i]
            outside = (at_leaf < 0) | (at_leaf >= leaves)
            off_chip = jnp.where(odd == 1, at_leaf >= leaves, at_leaf < 0)
            which = jnp.where(off_chip, 1, 0)
            inside = jnp.where(at_leaf < 0, at_leaf + leaves, jnp.where(at_leaf >= leaves, at_leaf - leaves, at_leaf))
            at = jnp.where(off_chip, filled[1], filled[0])
            lists[which, 0, at] = i * slots + j
            lists[which, 1, at] = 256 * (inside + jnp.where(outside & ~off_chip, leaves, 0))
            lists[which, 2, at] = i
            return filled[0] + 1 - which, filled[1] + which

        return lax.fori_loop(0, count[i], slot_body, filled)

    zero = jnp.int32(0)
    filled = lax.fori_loop(0, leaves, leaf_body, (zero, zero))
    for w in range(2):
        groups = (filled[w] + BATCH - 1) // BATCH

        def fill(e, carry, w=w):
            lists[w, 0, e] = 0
            lists[w, 1, e] = 0
            lists[w, 2, e] = leaves
            return carry

        lax.fori_loop(filled[w], groups * BATCH, fill, 0)
        counts[w] = groups

    def couple():
        panels = source.shape[3]
        for c in range(ssems.shape[0]):
            wait_halves(source_factor, source, ssems, c)
            wait_halves(target_factor, target, tsems, c)
        for h in range(2):
            for g in range(2):
                gram[h, g] = nt(source[h].reshape(-1, panels), target[g].reshape(-1, panels)).astype(BF16)

    own_part(lists, counts, field, mate, near, acc, others, tiles, sems, osem, mate_here, msem, couple)


def local_kernel(step, lists, counts, field, mate, near, tail, _, acc, others, out, *scratch):
    *scratch, sem = scratch
    width = tail.shape[1]
    copy = pltpu.make_async_copy(tail, out.at[step - 1, :, pl.ds(out.shape[2] - width, width)], sem)
    copy.start()
    own_part(lists, counts, field, mate, near, acc, others, *scratch)
    copy.wait()


def others_part(lists, counts, tiles, outer, acc):
    run_list(lists, counts[1], 1, 0, tiles, outer, acc)


def first_others_kernel(lists, counts, tiles, outer, source, _, acc, x):
    others_part(lists, counts, tiles, outer, acc)
    accs = None
    for i in range(acc.shape[0] - 1):
        accs = project(source, accs, i, acc[i].astype(BF16))
    x[...] = jnp.concatenate(accs, axis=1)


def others_kernel(lists, counts, tiles, outer, factor, _, acc, x, source, sems):
    start_halves(factor, source, sems)
    others_part(lists, counts, tiles, outer, acc)
    parts = sems.shape[0]
    per = (acc.shape[0] - 1) // parts
    accs = None
    for c in range(parts):
        wait_halves(factor, source, sems, c)
        for i in range(c * per, c * per + per):
            accs = project(source, accs, i, acc[i].astype(BF16))
    x[...] = jnp.concatenate(accs, axis=1)


def last_others_kernel(lists, counts, tiles, outer, _, acc):
    others_part(lists, counts, tiles, outer, acc)


def pick(far_src, far_count, received, picked):
    own = lax.axis_index("panels")
    live = far_count[own]
    for k in range(picked.shape[0] // 16):
        block = received[far_src[k, own]]
        picked[16 * k : 16 * k + 16] = jnp.where(k < live, block, jnp.zeros_like(block))


def expand(target_factor, acc, picked, wide, tsems, use, passed):
    turned = picked[...].astype(F32).T.astype(BF16)
    excite = turned.shape[0] // 2
    parts = tsems.shape[0]
    per = wide.shape[3] // 256 // parts
    for c in range(parts):
        wait_halves(target_factor, wide, tsems, c)
        for i in range(c * per, c * per + per):
            cols = slice(256 * i, 256 * i + 256)
            value = acc[i]
            for h in range(2):
                value += jnp.dot(
                    turned[excite * h : excite * h + excite],
                    wide[h, :, :, cols].reshape(-1, 256),
                    preferred_element_type=F32,
                )
            use(cols, value)
        passed(c)


def far_kernel(
    step, far_src, far_count, dest, received, target_factor, gram_in, acc, x, _, field, send, out, tail,
    gram, picked, ready, wide, done, tsems, psems, gsem, osems,
):
    brought = pltpu.make_async_copy(gram_in, gram, gsem)
    brought.start()
    start_halves(target_factor, wide, tsems)
    pick(far_src, far_count, received, picked)
    excite = picked.shape[1] // 2
    brought.wait()
    parts = []
    for h in range(2):
        part = x[:, excite * h : excite * h + excite]
        for g in range(2):
            part += jnp.dot(
                gram[h, g], picked[:, excite * g : excite * g + excite], preferred_element_type=F32
            )
        parts.append(part)
    ready[...] = jnp.concatenate(parts, axis=1).astype(BF16)
    placed = place(dest, ready, send, psems)
    next(placed)

    kept = done.shape[1]

    def use(cols, value):
        if cols.start < kept:
            done[:, cols] = value
        else:
            tail[:, cols.start - kept : cols.stop - kept] = value
        field[:, cols] = value.astype(BF16)

    copies = []

    def passed(c):
        if c < osems.shape[0]:
            store_part(step, c, done, out, osems, copies)

    expand(target_factor, acc, picked, wide, tsems, use, passed)
    next(placed)
    for copy in copies:
        copy.wait()


def store_part(step, c, done, out, osems, copies):
    width = done.shape[1] // osems.shape[0]
    cols = pl.ds(width * c, width)
    copies.append(pltpu.make_async_copy(done.at[:, cols], out.at[step, :, cols], osems.at[c]))
    copies[-1].start()


def last_kernel(step, far_src, far_count, received, target_factor, acc, _, out, picked, wide, done, tsems, osems):
    start_halves(target_factor, wide, tsems)
    pick(far_src, far_count, received, picked)
    copies = []

    def use(cols, value):
        done[:, cols] = value

    expand(target_factor, acc, picked, wide, tsems, use, lambda c: store_part(step, c, done, out, osems, copies))
    for copy in copies:
        copy.wait()


def far_lists(far_src, far_count, own):
    rows, slots = far_src.shape
    live = jnp.arange(slots, dtype=jnp.int32)[None, :] < far_count[:, None]
    has = jnp.any((far_src == own) & live, axis=1)
    order = jnp.arange(rows, dtype=jnp.int32)
    rank = jnp.sum((has[None, :] & (order[None, :] < order[:, None])).astype(jnp.int32), axis=1)
    hit = has[None, :] & (rank[None, :] == jnp.arange(slots, dtype=jnp.int32)[:, None])
    dest = jnp.max(jnp.where(hit, order[None, :], -1), axis=1)
    return dest


def shards(
    excitation, near_tiles, near_offset, near_count, far_src, far_count, source_factor, target_factor
):
    excite, panels = excitation.shape
    leaves, near_slots, leaf = near_tiles.shape[:3]
    rows, slots = far_src.shape
    rank = source_factor.shape[1]
    count = lax.axis_size("panels")
    dest = far_lists(far_src, far_count, lax.axis_index("panels"))

    tile_total = leaves * near_slots
    near = streamed(near_tiles.reshape(tile_total, leaf, leaf))
    source_factor, target_factor = streamed(source_factor), streamed(target_factor)
    entries = tile_total + BATCH
    half = slots * rank // 2
    send_type = pltpu.HBM((rows, rank // 2, 2 * excite), BF16)
    field_type = jax.ShapeDtypeStruct((excite, panels), BF16)
    acc_type = pltpu.VMEM((leaves + 1, excite, leaf), F32)
    out_type = pltpu.HBM((ITERS, excite, panels), F32)
    tiles_type = pltpu.VMEM((entries, leaf, leaf), BF16)
    half_type = pltpu.VMEM((2, slots, rank // 2, panels), BF16)
    done_type = pltpu.VMEM((excite, panels), F32)
    picked_type = pltpu.VMEM((half, 2 * excite), BF16)
    x_type = pltpu.VMEM((half, 2 * excite), F32)
    gram_shape = (2, 2, half, half)
    dma = pltpu.SemaphoreType.DMA
    groups = entries // BATCH
    far_flops = 2 * slots * rank * panels * excite

    def call(kernel, out_shape, in_specs, out_specs, scratch, flops, name, aliases=None):
        return pl.pallas_call(
            kernel,
            out_shape=out_shape,
            in_specs=in_specs,
            out_specs=out_specs,
            scratch_shapes=scratch,
            input_output_aliases=aliases or {},
            compiler_params=params(),
            cost_estimate=cost(flops, 2**22),
            name=name,
        )

    outward = [(i, (i + 2 * (i % 2) - 1) % count) for i in range(count)]
    inward = [(i, i + 1 - 2 * (i % 2)) for i in range(count)]
    field = send = lists = counts = out = gram = None
    turned_src = far_src.T
    for step in range(ITERS):
        if step == 0:
            send, field = call(
                first_kernel, (send_type, field_type), [SMEM, ANY, ANY], (ANY, VMEM),
                [half_type, picked_type, dma((PARTS, 2)), dma((slots,)), dma], far_flops, "first",
            )(dest, streamed(excitation), source_factor)
        outer = lax.ppermute(field, "panels", outward)
        mate = lax.ppermute(field, "panels", inward)
        received = lax.all_to_all(send, "panels", split_axis=0, concat_axis=0, tiled=True)
        own_scratch = [tiles_type, dma((groups,)), dma, pltpu.VMEM((excite, 2 * panels), BF16), dma((2,))]
        if step == 0:
            acc, tiles, source, gram, lists, counts, out = call(
                setup_kernel,
                (
                    acc_type, tiles_type, half_type, pltpu.HBM(gram_shape, BF16),
                    jax.ShapeDtypeStruct((2, 3, entries), jnp.int32),
                    jax.ShapeDtypeStruct((2,), jnp.int32),
                    out_type,
                ),
                [SMEM, SMEM, ANY, ANY, ANY, ANY, ANY], (VMEM, VMEM, VMEM, VMEM, SMEM, SMEM, ANY),
                [*own_scratch, half_type, dma((PARTS, 2)), dma((PARTS, 2))],
                tile_total * 2**22, "setup",
            )(near_offset.T, near_count, field, mate, near, source_factor, target_factor)
        else:
            acc, tiles, out = call(
                lambda *refs, step=step: local_kernel(step, *refs), (acc_type, tiles_type, out_type),
                [SMEM, SMEM, ANY, ANY, ANY, VMEM, ANY], (VMEM, VMEM, ANY), [*own_scratch, dma],
                tile_total * 2**22, "local", {6: 2},
            )(lists, counts, field, mate, near, pinned(tail), streamed(out))
        near_operands = (lists, counts, pinned(tiles), outer)
        if step == ITERS - 1:
            acc = call(
                last_others_kernel, acc_type, [SMEM, SMEM, VMEM, VMEM, VMEM], VMEM,
                [], tile_total * 2**22, "others", {4: 0},
            )(*near_operands, pinned(acc))
            return call(
                lambda *refs, step=step: last_kernel(step, *refs),
                out_type, [SMEM, SMEM, VMEM, ANY, VMEM, ANY], ANY,
                [picked_type, half_type, done_type, dma((PARTS, 2)), dma((PARTS,))],
                far_flops, "last", {5: 0},
            )(turned_src, far_count, received, target_factor, pinned(acc), streamed(out))
        if step == 0:
            acc, x = call(
                first_others_kernel, (acc_type, x_type), [SMEM, SMEM, VMEM, VMEM, VMEM, VMEM], (VMEM, VMEM),
                [], tile_total * 2**22, "others", {5: 0},
            )(*near_operands, pinned(source), pinned(acc))
        else:
            acc, x = call(
                others_kernel, (acc_type, x_type), [SMEM, SMEM, VMEM, VMEM, ANY, VMEM], (VMEM, VMEM),
                [half_type, dma((PARTS, 2))], tile_total * 2**22, "others", {5: 0},
            )(*near_operands, source_factor, pinned(acc))
        width = panels // PARTS
        field, send, out, tail = call(
            lambda *refs, step=step: far_kernel(step, *refs),
            (field_type, send_type, out_type, pltpu.VMEM((excite, width), F32)),
            [SMEM, SMEM, SMEM, VMEM, ANY, ANY, VMEM, VMEM, ANY], (VMEM, ANY, ANY, VMEM),
            [
                pltpu.VMEM(gram_shape, BF16), picked_type, picked_type, half_type,
                pltpu.VMEM((excite, panels - width), F32),
                dma((PARTS, 2)), dma((slots,)), dma, dma((PARTS - 1,)),
            ],
            far_flops, "far", {8: 2},
        )(
            turned_src, far_count, dest, received, target_factor, streamed(gram), pinned(acc), pinned(x),
            streamed(out),
        )


def solution(mesh):
    in_specs = (
        P(None, "panels"),
        P("panels", None, None, None),
        P("panels", None),
        P("panels"),
        P(),
        P(),
        P(None, None, "panels"),
        P(None, None, "panels"),
    )
    out_specs = P(None, None, "panels")
    return jax.shard_map(shards, mesh=mesh, in_specs=in_specs, out_specs=out_specs, check_vma=False)
```

```python
import jax
import jax.numpy as jnp
from jax import lax
from jax.experimental import pallas as pl
from jax.experimental.pallas import tpu as pltpu
from jax.sharding import PartitionSpec as P

ITERS = 5
BATCH = 8
PARTS = 4
KEPT = 2
F32 = jnp.float32
BF16 = jnp.bfloat16
NT = (((1,), (1,)), ((), ()))
VMEM = pl.BlockSpec(memory_space=pltpu.VMEM)
SMEM = pl.BlockSpec(memory_space=pltpu.SMEM)
ANY = pl.BlockSpec(memory_space=pl.ANY)
LIMIT = 24 * 2**20


def nt(a, b):
    return lax.dot_general(a, b, NT, preferred_element_type=F32)


def pinned(x):
    return pltpu.with_memory_space_constraint(x, pltpu.VMEM)


def streamed(x):
    return pltpu.with_memory_space_constraint(x, pltpu.HBM)


def params():
    return pltpu.CompilerParams(vmem_limit_bytes=LIMIT)


def cost(flops, touched):
    return pl.CostEstimate(flops=flops, bytes_accessed=touched, transcendentals=0)


def place(dest, x, send, sem):
    slots = x.shape[0] // 16

    def copy(q):
        return pltpu.make_async_copy(x.at[pl.ds(16 * q, 16)], send.at[dest[q]], sem.at[q])

    for act in ("start", "wait"):
        for q in range(slots):

            @pl.when(dest[q] >= 0)
            def _():
                getattr(copy(q), act)()

        if act == "start":
            yield
    yield


def project(source, accs, i, leaf):
    out = []
    for h in range(2):
        part = source[h, :, :, 256 * i : 256 * i + 256]
        term = nt(part.reshape(-1, 256), leaf)
        out.append(term if accs is None else accs[h] + term)
    return out


def half_copy(factor, wide, sems, c, h):
    width = wide.shape[3] // sems.shape[0]
    cols = pl.ds(c * width, width)
    return pltpu.make_async_copy(factor.at[:, pl.ds(16 * h, 16), cols], wide.at[h, :, :, cols], sems.at[c, h])


def start_halves(factor, wide, sems):
    for c in range(sems.shape[0]):
        for h in range(2):
            half_copy(factor, wide, sems, c, h).start()


def wait_halves(factor, wide, sems, c):
    for h in range(2):
        half_copy(factor, wide, sems, c, h).wait()


def first_kernel(dest, field_in, factor, send, field, source, x, sems, psem, fsem):
    brought = pltpu.make_async_copy(field_in, field, fsem)
    brought.start()
    start_halves(factor, source, sems)
    brought.wait()
    parts = sems.shape[0]
    per = field.shape[1] // 256 // parts
    accs = None
    for c in range(parts):
        wait_halves(factor, source, sems, c)
        for i in range(c * per, c * per + per):
            accs = project(source, accs, i, field[:, 256 * i : 256 * i + 256])
    x[...] = jnp.concatenate(accs, axis=1).astype(BF16)
    for _ in place(dest, x, send, psem):
        pass


def fetch_list(lists, groups, which, base, near, tiles, sem_of):
    def body(g, carry):
        for b in range(BATCH):
            e = g * BATCH + b
            pltpu.make_async_copy(near.at[lists[which, 0, e]], tiles.at[base + e], sem_of(g)).start()
        return carry

    lax.fori_loop(0, groups, body, 0)


def arrived(near, tiles, sem, at):
    pltpu.make_async_copy(near.at[pl.ds(0, BATCH)], tiles.at[pl.ds(at, BATCH)], sem).wait()


def run_list(lists, groups, which, base, tiles, field, acc, ready=None):
    def body(g, carry):
        if ready is not None:
            ready(g)
        found = []
        for b in range(BATCH):
            e = g * BATCH + b
            at = pl.multiple_of(lists[which, 1, e], 256)
            found.append(nt(field[:, pl.ds(at, 256)], tiles[base + e]))
        for b in range(BATCH):
            e = g * BATCH + b
            acc[lists[which, 2, e]] += found[b]
        return carry

    lax.fori_loop(0, groups, body, 0)


def own_part(lists, counts, field, mate, near, acc, others, tiles, sems, osem, both, bsems, between=None):
    panels = field.shape[1]
    brought = [
        pltpu.make_async_copy(part, both.at[:, pl.ds(panels * k, panels)], bsems.at[k])
        for k, part in enumerate((field, mate))
    ]
    for copy in brought:
        copy.start()
    fetch_list(lists, counts[0], 0, 0, near, tiles, lambda g: sems.at[g])
    fetch_list(lists, counts[1], 1, 0, near, others, lambda g: osem)
    if between is not None:
        between()
    acc[...] = jnp.zeros_like(acc)
    for copy in brought:
        copy.wait()

    def ready(g):
        arrived(near, tiles, sems.at[g], g * BATCH)

    run_list(lists, counts[0], 0, 0, tiles, both, acc, ready)

    def body(g, carry):
        arrived(near, others, osem, g * BATCH)
        return carry

    lax.fori_loop(0, counts[1], body, 0)


def setup_kernel(
    offset, count, field, mate, near, source_factor, target_factor,
    acc, others, source, gram, lists, counts, out, tiles, sems, osem, mate_here, msem, target, ssems, tsems,
):
    leaves = count.shape[0]
    slots = near.shape[0] // leaves
    odd = lax.axis_index("panels") % 2

    def leaf_body(i, filled):
        def slot_body(j, filled):
            at_leaf = i + offset[j, i]
            outside = (at_leaf < 0) | (at_leaf >= leaves)
            off_chip = jnp.where(odd == 1, at_leaf >= leaves, at_leaf < 0)
            which = jnp.where(off_chip, 1, 0)
            inside = jnp.where(at_leaf < 0, at_leaf + leaves, jnp.where(at_leaf >= leaves, at_leaf - leaves, at_leaf))
            at = jnp.where(off_chip, filled[1], filled[0])
            lists[which, 0, at] = i * slots + j
            lists[which, 1, at] = 256 * (inside + jnp.where(outside & ~off_chip, leaves, 0))
            lists[which, 2, at] = i
            return filled[0] + 1 - which, filled[1] + which

        return lax.fori_loop(0, count[i], slot_body, filled)

    zero = jnp.int32(0)
    filled = lax.fori_loop(0, leaves, leaf_body, (zero, zero))
    for w in range(2):
        groups = (filled[w] + BATCH - 1) // BATCH

        def fill(e, carry, w=w):
            lists[w, 0, e] = 0
            lists[w, 1, e] = 0
            lists[w, 2, e] = leaves
            return carry

        lax.fori_loop(filled[w], groups * BATCH, fill, 0)
        counts[w] = groups

    def start_factors():
        start_halves(source_factor, source, ssems)
        start_halves(target_factor, target, tsems)

    own_part(lists, counts, field, mate, near, acc, others, tiles, sems, osem, mate_here, msem, start_factors)
    panels = source.shape[3]
    for c in range(ssems.shape[0]):
        wait_halves(source_factor, source, ssems, c)
        wait_halves(target_factor, target, tsems, c)
    for h in range(2):
        for g in range(2):
            gram[h, g] = nt(source[h].reshape(-1, panels), target[g].reshape(-1, panels)).astype(BF16)


def store_tail(step, tail, out, sem):
    width = tail.shape[1]
    return pltpu.make_async_copy(tail, out.at[step - 1, :, pl.ds(out.shape[2] - width, width)], sem)


def local_kernel(
    step, lists, counts, field, mate, near, factor, tail, _, acc, others, source, out,
    tiles, sems, osem, both, bsems, sem, ssems,
):
    copy = store_tail(step, tail, out, sem)
    copy.start()
    own_part(
        lists, counts, field, mate, near, acc, others, tiles, sems, osem, both, bsems,
        lambda: start_halves(factor, source, ssems),
    )
    for c in range(ssems.shape[0]):
        wait_halves(factor, source, ssems, c)
    copy.wait()


def last_local_kernel(step, lists, counts, field, mate, near, tail, _, acc, others, out, *scratch):
    *scratch, sem = scratch
    copy = store_tail(step, tail, out, sem)
    copy.start()
    own_part(lists, counts, field, mate, near, acc, others, *scratch)
    copy.wait()


def others_part(lists, counts, tiles, outer, acc):
    run_list(lists, counts[1], 1, 0, tiles, outer, acc)


def others_kernel(lists, counts, tiles, outer, source, _, acc, x):
    others_part(lists, counts, tiles, outer, acc)
    accs = None
    for i in range(acc.shape[0] - 1):
        accs = project(source, accs, i, acc[i].astype(BF16))
    x[...] = jnp.concatenate(accs, axis=1)


def last_others_kernel(lists, counts, tiles, outer, _, acc):
    others_part(lists, counts, tiles, outer, acc)


def pick(far_src, far_count, received, picked):
    own = lax.axis_index("panels")
    live = far_count[own]
    for k in range(picked.shape[0] // 16):
        block = received[far_src[k, own]]
        picked[16 * k : 16 * k + 16] = jnp.where(k < live, block, jnp.zeros_like(block))


def expand(target_factor, acc, picked, wide, tsems, use, passed):
    turned = picked[...].astype(F32).T.astype(BF16)
    excite = turned.shape[0] // 2
    parts = tsems.shape[0]
    per = wide.shape[3] // 256 // parts
    for c in range(parts):
        wait_halves(target_factor, wide, tsems, c)
        for i in range(c * per, c * per + per):
            cols = slice(256 * i, 256 * i + 256)
            value = acc[i]
            for h in range(2):
                value += jnp.dot(
                    turned[excite * h : excite * h + excite],
                    wide[h, :, :, cols].reshape(-1, 256),
                    preferred_element_type=F32,
                )
            use(cols, value)
        passed(c)


def far_kernel(
    step, far_src, far_count, dest, received, target_factor, gram_in, acc, x, _, field, send, out, tail,
    gram, picked, ready, wide, done, tsems, psems, gsem, osems,
):
    brought = pltpu.make_async_copy(gram_in, gram, gsem)
    brought.start()
    start_halves(target_factor, wide, tsems)
    pick(far_src, far_count, received, picked)
    excite = picked.shape[1] // 2
    brought.wait()
    parts = []
    for h in range(2):
        part = x[:, excite * h : excite * h + excite]
        for g in range(2):
            part += jnp.dot(
                gram[h, g], picked[:, excite * g : excite * g + excite], preferred_element_type=F32
            )
        parts.append(part)
    ready[...] = jnp.concatenate(parts, axis=1).astype(BF16)
    placed = place(dest, ready, send, psems)
    next(placed)

    kept = done.shape[1]

    def use(cols, value):
        if cols.start < kept:
            done[:, cols] = value
        else:
            tail[:, cols.start - kept : cols.stop - kept] = value
        field[:, cols] = value.astype(BF16)

    copies = []

    def passed(c):
        if c < osems.shape[0]:
            store_part(step, c, done, out, osems, copies)

    expand(target_factor, acc, picked, wide, tsems, use, passed)
    next(placed)
    for copy in copies:
        copy.wait()


def store_part(step, c, done, out, osems, copies):
    width = done.shape[1] // osems.shape[0]
    cols = pl.ds(width * c, width)
    copies.append(pltpu.make_async_copy(done.at[:, cols], out.at[step, :, cols], osems.at[c]))
    copies[-1].start()


def last_kernel(step, far_src, far_count, received, target_factor, acc, _, out, picked, wide, done, tsems, osems):
    start_halves(target_factor, wide, tsems)
    pick(far_src, far_count, received, picked)
    copies = []

    def use(cols, value):
        done[:, cols] = value

    expand(target_factor, acc, picked, wide, tsems, use, lambda c: store_part(step, c, done, out, osems, copies))
    for copy in copies:
        copy.wait()


def far_lists(far_src, far_count, own):
    rows, slots = far_src.shape
    live = jnp.arange(slots, dtype=jnp.int32)[None, :] < far_count[:, None]
    has = jnp.any((far_src == own) & live, axis=1)
    order = jnp.arange(rows, dtype=jnp.int32)
    rank = jnp.sum((has[None, :] & (order[None, :] < order[:, None])).astype(jnp.int32), axis=1)
    hit = has[None, :] & (rank[None, :] == jnp.arange(slots, dtype=jnp.int32)[:, None])
    dest = jnp.max(jnp.where(hit, order[None, :], -1), axis=1)
    return dest


def shards(
    excitation, near_tiles, near_offset, near_count, far_src, far_count, source_factor, target_factor
):
    excite, panels = excitation.shape
    leaves, near_slots, leaf = near_tiles.shape[:3]
    rows, slots = far_src.shape
    rank = source_factor.shape[1]
    count = lax.axis_size("panels")
    dest = far_lists(far_src, far_count, lax.axis_index("panels"))

    tile_total = leaves * near_slots
    near = streamed(near_tiles.reshape(tile_total, leaf, leaf))
    source_factor, target_factor = streamed(source_factor), streamed(target_factor)
    entries = tile_total + BATCH
    half = slots * rank // 2
    send_type = pltpu.HBM((rows, rank // 2, 2 * excite), BF16)
    field_type = jax.ShapeDtypeStruct((excite, panels), BF16)
    acc_type = pltpu.VMEM((leaves + 1, excite, leaf), F32)
    out_type = pltpu.HBM((ITERS, excite, panels), F32)
    tiles_type = pltpu.VMEM((entries, leaf, leaf), BF16)
    half_type = pltpu.VMEM((2, slots, rank // 2, panels), BF16)
    done_type = pltpu.VMEM((excite, panels), F32)
    picked_type = pltpu.VMEM((half, 2 * excite), BF16)
    x_type = pltpu.VMEM((half, 2 * excite), F32)
    gram_shape = (2, 2, half, half)
    dma = pltpu.SemaphoreType.DMA
    groups = entries // BATCH
    far_flops = 2 * slots * rank * panels * excite

    def call(kernel, out_shape, in_specs, out_specs, scratch, flops, name, aliases=None):
        return pl.pallas_call(
            kernel,
            out_shape=out_shape,
            in_specs=in_specs,
            out_specs=out_specs,
            scratch_shapes=scratch,
            input_output_aliases=aliases or {},
            compiler_params=params(),
            cost_estimate=cost(flops, 2**22),
            name=name,
        )

    outward = [(i, (i + 2 * (i % 2) - 1) % count) for i in range(count)]
    inward = [(i, i + 1 - 2 * (i % 2)) for i in range(count)]
    field = send = lists = counts = out = gram = None
    turned_src = far_src.T
    for step in range(ITERS):
        if step == 0:
            send, field = call(
                first_kernel, (send_type, field_type), [SMEM, ANY, ANY], (ANY, VMEM),
                [half_type, picked_type, dma((PARTS, 2)), dma((slots,)), dma], far_flops, "first",
            )(dest, streamed(excitation), source_factor)
        outer = lax.ppermute(field, "panels", outward)
        mate = lax.ppermute(field, "panels", inward)
        received = lax.all_to_all(send, "panels", split_axis=0, concat_axis=0, tiled=True)
        own_scratch = [tiles_type, dma((groups,)), dma, pltpu.VMEM((excite, 2 * panels), BF16), dma((2,))]
        if step == 0:
            acc, tiles, source, gram, lists, counts, out = call(
                setup_kernel,
                (
                    acc_type, tiles_type, half_type, pltpu.HBM(gram_shape, BF16),
                    jax.ShapeDtypeStruct((2, 3, entries), jnp.int32),
                    jax.ShapeDtypeStruct((2,), jnp.int32),
                    out_type,
                ),
                [SMEM, SMEM, ANY, ANY, ANY, ANY, ANY], (VMEM, VMEM, VMEM, VMEM, SMEM, SMEM, ANY),
                [*own_scratch, half_type, dma((PARTS, 2)), dma((PARTS, 2))],
                tile_total * 2**22, "setup",
            )(near_offset.T, near_count, field, mate, near, source_factor, target_factor)
        else:
            last = step == ITERS - 1
            acc, tiles, *source, out = call(
                lambda *refs, step=step, last=last: (last_local_kernel if last else local_kernel)(step, *refs),
                (acc_type, tiles_type, *([] if last else [half_type]), out_type),
                [SMEM, SMEM, ANY, ANY, ANY, *([] if last else [ANY]), VMEM, ANY],
                (VMEM, VMEM, *([] if last else [VMEM]), ANY),
                [*own_scratch, dma, *([] if last else [dma((PARTS, 2))])],
                tile_total * 2**22, "local", {6: 2} if last else {7: 3},
            )(
                lists, counts, field, mate, near, *([] if last else [source_factor]),
                pinned(tail), streamed(out),
            )
            source = None if last else source[0]
        near_operands = (lists, counts, pinned(tiles), outer)
        if step == ITERS - 1:
            acc = call(
                last_others_kernel, acc_type, [SMEM, SMEM, VMEM, VMEM, VMEM], VMEM,
                [], tile_total * 2**22, "others", {4: 0},
            )(*near_operands, pinned(acc))
            return call(
                lambda *refs, step=step: last_kernel(step, *refs),
                out_type, [SMEM, SMEM, VMEM, ANY, VMEM, ANY], ANY,
                [picked_type, half_type, done_type, dma((PARTS, 2)), dma((PARTS,))],
                far_flops, "last", {5: 0},
            )(turned_src, far_count, received, target_factor, pinned(acc), streamed(out))
        acc, x = call(
            others_kernel, (acc_type, x_type), [SMEM, SMEM, VMEM, VMEM, VMEM, VMEM], (VMEM, VMEM),
            [], tile_total * 2**22, "others", {5: 0},
        )(*near_operands, pinned(source), pinned(acc))
        width = panels // PARTS * KEPT
        field, send, out, tail = call(
            lambda *refs, step=step: far_kernel(step, *refs),
            (field_type, send_type, out_type, pltpu.VMEM((excite, width), F32)),
            [SMEM, SMEM, SMEM, VMEM, ANY, ANY, VMEM, VMEM, ANY], (VMEM, ANY, ANY, VMEM),
            [
                pltpu.VMEM(gram_shape, BF16), picked_type, picked_type, half_type,
                pltpu.VMEM((excite, panels - width), F32),
                dma((PARTS, 2)), dma((slots,)), dma, dma((PARTS - KEPT,)),
            ],
            far_flops, "far", {8: 2},
        )(
            turned_src, far_count, dest, received, target_factor, streamed(gram), pinned(acc), pinned(x),
            streamed(out),
        )


def solution(mesh):
    in_specs = (
        P(None, "panels"),
        P("panels", None, None, None),
        P("panels", None),
        P("panels"),
        P(),
        P(),
        P(None, None, "panels"),
        P(None, None, "panels"),
    )
    out_specs = P(None, None, "panels")
    return jax.shard_map(shards, mesh=mesh, in_specs=in_specs, out_specs=out_specs, check_vma=False)
```

```python
import jax
import jax.numpy as jnp
from jax import lax
from jax.experimental import pallas as pl
from jax.experimental.pallas import tpu as pltpu
from jax.sharding import PartitionSpec as P

ITERS = 5
BATCH = 8
PARTS = 4
KEPT = 2
F32 = jnp.float32
BF16 = jnp.bfloat16
NT = (((1,), (1,)), ((), ()))
VMEM = pl.BlockSpec(memory_space=pltpu.VMEM)
SMEM = pl.BlockSpec(memory_space=pltpu.SMEM)
ANY = pl.BlockSpec(memory_space=pl.ANY)
LIMIT = 24 * 2**20


def nt(a, b):
    return lax.dot_general(a, b, NT, preferred_element_type=F32)


def pinned(x):
    return pltpu.with_memory_space_constraint(x, pltpu.VMEM)


def streamed(x):
    return pltpu.with_memory_space_constraint(x, pltpu.HBM)


def params():
    return pltpu.CompilerParams(vmem_limit_bytes=LIMIT)


def cost(flops, touched):
    return pl.CostEstimate(flops=flops, bytes_accessed=touched, transcendentals=0)


def place(dest, x, send, sem):
    slots = x.shape[0] // 16

    def copy(q):
        return pltpu.make_async_copy(x.at[pl.ds(16 * q, 16)], send.at[dest[q]], sem.at[q])

    for act in ("start", "wait"):
        for q in range(slots):

            @pl.when(dest[q] >= 0)
            def _():
                getattr(copy(q), act)()

        if act == "start":
            yield
    yield


def project(source, accs, i, leaf):
    out = []
    for h in range(2):
        part = source[h, :, :, 256 * i : 256 * i + 256]
        term = nt(part.reshape(-1, 256), leaf)
        out.append(term if accs is None else accs[h] + term)
    return out


def half_copy(factor, wide, sems, c, h):
    width = wide.shape[3] // sems.shape[0]
    cols = pl.ds(c * width, width)
    return pltpu.make_async_copy(factor.at[:, pl.ds(16 * h, 16), cols], wide.at[h, :, :, cols], sems.at[c, h])


def start_halves(factor, wide, sems):
    for c in range(sems.shape[0]):
        for h in range(2):
            half_copy(factor, wide, sems, c, h).start()


def wait_halves(factor, wide, sems, c):
    for h in range(2):
        half_copy(factor, wide, sems, c, h).wait()


def first_kernel(dest, field_in, factor, send, field, source, x, sems, psem, fsem):
    brought = pltpu.make_async_copy(field_in, field, fsem)
    brought.start()
    start_halves(factor, source, sems)
    brought.wait()
    parts = sems.shape[0]
    per = field.shape[1] // 256 // parts
    accs = None
    for c in range(parts):
        wait_halves(factor, source, sems, c)
        for i in range(c * per, c * per + per):
            accs = project(source, accs, i, field[:, 256 * i : 256 * i + 256])
    x[...] = jnp.concatenate(accs, axis=1).astype(BF16)
    for _ in place(dest, x, send, psem):
        pass


def fetch_list(lists, groups, which, base, near, tiles, sem_of):
    def body(g, carry):
        for b in range(BATCH):
            e = g * BATCH + b
            pltpu.make_async_copy(near.at[lists[which, 0, e]], tiles.at[base + e], sem_of(g)).start()
        return carry

    lax.fori_loop(0, groups, body, 0)


def arrived(near, tiles, sem, at):
    pltpu.make_async_copy(near.at[pl.ds(0, BATCH)], tiles.at[pl.ds(at, BATCH)], sem).wait()


def run_list(lists, groups, which, base, tiles, field, acc, ready=None):
    def body(g, carry):
        if ready is not None:
            ready(g)
        found = []
        for b in range(BATCH):
            e = g * BATCH + b
            at = pl.multiple_of(lists[which, 1, e], 256)
            found.append(nt(field[:, pl.ds(at, 256)], tiles[base + e]))
        for b in range(BATCH):
            e = g * BATCH + b
            acc[lists[which, 2, e]] += found[b]
        return carry

    lax.fori_loop(0, groups, body, 0)


def own_part(lists, counts, field, mate, near, acc, others, tiles, sems, osem, both, bsems, between=None):
    panels = field.shape[1]
    brought = [
        pltpu.make_async_copy(part, both.at[:, pl.ds(panels * k, panels)], bsems.at[k])
        for k, part in enumerate((field, mate))
    ]
    for copy in brought:
        copy.start()
    fetch_list(lists, counts[0], 0, 0, near, tiles, lambda g: sems.at[g])
    fetch_list(lists, counts[1], 1, 0, near, others, lambda g: osem)
    if between is not None:
        between()
    acc[...] = jnp.zeros_like(acc)
    for copy in brought:
        copy.wait()

    def ready(g):
        arrived(near, tiles, sems.at[g], g * BATCH)

    run_list(lists, counts[0], 0, 0, tiles, both, acc, ready)

    def body(g, carry):
        arrived(near, others, osem, g * BATCH)
        return carry

    lax.fori_loop(0, counts[1], body, 0)


def setup_kernel(
    offset, count, field, mate, near, source_factor, target_factor,
    acc, others, source, gram, lists, counts, out, tiles, sems, osem, mate_here, msem, target, ssems, tsems,
):
    start_halves(source_factor, source, ssems)
    start_halves(target_factor, target, tsems)
    leaves = count.shape[0]
    slots = near.shape[0] // leaves
    odd = lax.axis_index("panels") % 2

    def leaf_body(i, filled):
        def slot_body(j, filled):
            at_leaf = i + offset[j, i]
            outside = (at_leaf < 0) | (at_leaf >= leaves)
            off_chip = jnp.where(odd == 1, at_leaf >= leaves, at_leaf < 0)
            which = jnp.where(off_chip, 1, 0)
            inside = jnp.where(at_leaf < 0, at_leaf + leaves, jnp.where(at_leaf >= leaves, at_leaf - leaves, at_leaf))
            at = jnp.where(off_chip, filled[1], filled[0])
            lists[which, 0, at] = i * slots + j
            lists[which, 1, at] = 256 * (inside + jnp.where(outside & ~off_chip, leaves, 0))
            lists[which, 2, at] = i
            return filled[0] + 1 - which, filled[1] + which

        return lax.fori_loop(0, count[i], slot_body, filled)

    zero = jnp.int32(0)
    filled = lax.fori_loop(0, leaves, leaf_body, (zero, zero))
    for w in range(2):
        groups = (filled[w] + BATCH - 1) // BATCH

        def fill(e, carry, w=w):
            lists[w, 0, e] = 0
            lists[w, 1, e] = 0
            lists[w, 2, e] = leaves
            return carry

        lax.fori_loop(filled[w], groups * BATCH, fill, 0)
        counts[w] = groups

    def couple():
        panels = source.shape[3]
        for c in range(ssems.shape[0]):
            wait_halves(source_factor, source, ssems, c)
            wait_halves(target_factor, target, tsems, c)
        for h in range(2):
            for g in range(2):
                gram[h, g] = nt(source[h].reshape(-1, panels), target[g].reshape(-1, panels)).astype(BF16)

    own_part(lists, counts, field, mate, near, acc, others, tiles, sems, osem, mate_here, msem, couple)


def store_tail(step, tail, out, sem):
    width = tail.shape[1]
    return pltpu.make_async_copy(tail, out.at[step - 1, :, pl.ds(out.shape[2] - width, width)], sem)


def local_kernel(
    step, lists, counts, field, mate, near, factor, tail, _, acc, others, source, out,
    tiles, sems, osem, both, bsems, sem, ssems,
):
    copy = store_tail(step, tail, out, sem)
    copy.start()
    own_part(
        lists, counts, field, mate, near, acc, others, tiles, sems, osem, both, bsems,
        lambda: start_halves(factor, source, ssems),
    )
    for c in range(ssems.shape[0]):
        wait_halves(factor, source, ssems, c)
    copy.wait()


def last_local_kernel(step, lists, counts, field, mate, near, tail, _, acc, others, out, *scratch):
    *scratch, sem = scratch
    copy = store_tail(step, tail, out, sem)
    copy.start()
    own_part(lists, counts, field, mate, near, acc, others, *scratch)
    copy.wait()


def others_part(lists, counts, tiles, outer, acc):
    run_list(lists, counts[1], 1, 0, tiles, outer, acc)


def others_kernel(lists, counts, tiles, outer, source, _, acc, x):
    others_part(lists, counts, tiles, outer, acc)
    accs = None
    for i in range(acc.shape[0] - 1):
        accs = project(source, accs, i, acc[i].astype(BF16))
    x[...] = jnp.concatenate(accs, axis=1)


def last_others_kernel(lists, counts, tiles, outer, _, acc):
    others_part(lists, counts, tiles, outer, acc)


def pick(far_src, far_count, received, picked):
    own = lax.axis_index("panels")
    live = far_count[own]
    for k in range(picked.shape[0] // 16):
        block = received[far_src[k, own]]
        picked[16 * k : 16 * k + 16] = jnp.where(k < live, block, jnp.zeros_like(block))


def expand(target_factor, acc, picked, wide, tsems, use, passed):
    turned = picked[...].astype(F32).T.astype(BF16)
    excite = turned.shape[0] // 2
    parts = tsems.shape[0]
    per = wide.shape[3] // 256 // parts
    for c in range(parts):
        wait_halves(target_factor, wide, tsems, c)
        for i in range(c * per, c * per + per):
            cols = slice(256 * i, 256 * i + 256)
            value = acc[i]
            for h in range(2):
                value += jnp.dot(
                    turned[excite * h : excite * h + excite],
                    wide[h, :, :, cols].reshape(-1, 256),
                    preferred_element_type=F32,
                )
            use(cols, value)
        passed(c)


def far_kernel(
    step, far_src, far_count, dest, received, target_factor, gram_in, acc, x, _, field, send, out, tail,
    gram, picked, ready, wide, done, tsems, psems, gsem, osems,
):
    brought = pltpu.make_async_copy(gram_in, gram, gsem)
    brought.start()
    start_halves(target_factor, wide, tsems)
    pick(far_src, far_count, received, picked)
    excite = picked.shape[1] // 2
    brought.wait()
    parts = []
    for h in range(2):
        part = x[:, excite * h : excite * h + excite]
        for g in range(2):
            part += jnp.dot(
                gram[h, g], picked[:, excite * g : excite * g + excite], preferred_element_type=F32
            )
        parts.append(part)
    ready[...] = jnp.concatenate(parts, axis=1).astype(BF16)
    placed = place(dest, ready, send, psems)
    next(placed)

    kept = done.shape[1]

    def use(cols, value):
        if cols.start < kept:
            done[:, cols] = value
        else:
            tail[:, cols.start - kept : cols.stop - kept] = value
        field[:, cols] = value.astype(BF16)

    copies = []

    def passed(c):
        if c < osems.shape[0]:
            store_part(step, c, done, out, osems, copies)

    expand(target_factor, acc, picked, wide, tsems, use, passed)
    next(placed)
    for copy in copies:
        copy.wait()


def store_part(step, c, done, out, osems, copies):
    width = done.shape[1] // osems.shape[0]
    cols = pl.ds(width * c, width)
    copies.append(pltpu.make_async_copy(done.at[:, cols], out.at[step, :, cols], osems.at[c]))
    copies[-1].start()


def last_kernel(step, far_src, far_count, received, target_factor, acc, _, out, picked, wide, done, tsems, osems):
    start_halves(target_factor, wide, tsems)
    pick(far_src, far_count, received, picked)
    copies = []

    def use(cols, value):
        done[:, cols] = value

    expand(target_factor, acc, picked, wide, tsems, use, lambda c: store_part(step, c, done, out, osems, copies))
    for copy in copies:
        copy.wait()


def far_lists(far_src, far_count, own):
    rows, slots = far_src.shape
    live = jnp.arange(slots, dtype=jnp.int32)[None, :] < far_count[:, None]
    has = jnp.any((far_src == own) & live, axis=1)
    order = jnp.arange(rows, dtype=jnp.int32)
    rank = jnp.sum((has[None, :] & (order[None, :] < order[:, None])).astype(jnp.int32), axis=1)
    hit = has[None, :] & (rank[None, :] == jnp.arange(slots, dtype=jnp.int32)[:, None])
    dest = jnp.max(jnp.where(hit, order[None, :], -1), axis=1)
    return dest


def shards(
    excitation, near_tiles, near_offset, near_count, far_src, far_count, source_factor, target_factor
):
    excite, panels = excitation.shape
    leaves, near_slots, leaf = near_tiles.shape[:3]
    rows, slots = far_src.shape
    rank = source_factor.shape[1]
    count = lax.axis_size("panels")
    dest = far_lists(far_src, far_count, lax.axis_index("panels"))

    tile_total = leaves * near_slots
    near = streamed(near_tiles.reshape(tile_total, leaf, leaf))
    source_factor, target_factor = streamed(source_factor), streamed(target_factor)
    entries = tile_total + BATCH
    half = slots * rank // 2
    send_type = pltpu.HBM((rows, rank // 2, 2 * excite), BF16)
    field_type = jax.ShapeDtypeStruct((excite, panels), BF16)
    acc_type = pltpu.VMEM((leaves + 1, excite, leaf), F32)
    out_type = pltpu.HBM((ITERS, excite, panels), F32)
    tiles_type = pltpu.VMEM((entries, leaf, leaf), BF16)
    half_type = pltpu.VMEM((2, slots, rank // 2, panels), BF16)
    done_type = pltpu.VMEM((excite, panels), F32)
    picked_type = pltpu.VMEM((half, 2 * excite), BF16)
    x_type = pltpu.VMEM((half, 2 * excite), F32)
    gram_shape = (2, 2, half, half)
    dma = pltpu.SemaphoreType.DMA
    groups = entries // BATCH
    far_flops = 2 * slots * rank * panels * excite

    def call(kernel, out_shape, in_specs, out_specs, scratch, flops, name, aliases=None):
        return pl.pallas_call(
            kernel,
            out_shape=out_shape,
            in_specs=in_specs,
            out_specs=out_specs,
            scratch_shapes=scratch,
            input_output_aliases=aliases or {},
            compiler_params=params(),
            cost_estimate=cost(flops, 2**22),
            name=name,
        )

    outward = [(i, (i + 2 * (i % 2) - 1) % count) for i in range(count)]
    inward = [(i, i + 1 - 2 * (i % 2)) for i in range(count)]
    field = send = lists = counts = out = gram = None
    turned_src = far_src.T
    for step in range(ITERS):
        if step == 0:
            send, field = call(
                first_kernel, (send_type, field_type), [SMEM, ANY, ANY], (ANY, VMEM),
                [half_type, picked_type, dma((PARTS, 2)), dma((slots,)), dma], far_flops, "first",
            )(dest, streamed(excitation), source_factor)
        outer = lax.ppermute(field, "panels", outward)
        mate = lax.ppermute(field, "panels", inward)
        received = lax.all_to_all(send, "panels", split_axis=0, concat_axis=0, tiled=True)
        own_scratch = [tiles_type, dma((groups,)), dma, pltpu.VMEM((excite, 2 * panels), BF16), dma((2,))]
        if step == 0:
            acc, tiles, source, gram, lists, counts, out = call(
                setup_kernel,
                (
                    acc_type, tiles_type, half_type, pltpu.HBM(gram_shape, BF16),
                    jax.ShapeDtypeStruct((2, 3, entries), jnp.int32),
                    jax.ShapeDtypeStruct((2,), jnp.int32),
                    out_type,
                ),
                [SMEM, SMEM, ANY, ANY, ANY, ANY, ANY], (VMEM, VMEM, VMEM, VMEM, SMEM, SMEM, ANY),
                [*own_scratch, half_type, dma((PARTS, 2)), dma((PARTS, 2))],
                tile_total * 2**22, "setup",
            )(near_offset.T, near_count, field, mate, near, source_factor, target_factor)
        else:
            last = step == ITERS - 1
            acc, tiles, *source, out = call(
                lambda *refs, step=step, last=last: (last_local_kernel if last else local_kernel)(step, *refs),
                (acc_type, tiles_type, *([] if last else [half_type]), out_type),
                [SMEM, SMEM, ANY, ANY, ANY, *([] if last else [ANY]), VMEM, ANY],
                (VMEM, VMEM, *([] if last else [VMEM]), ANY),
                [*own_scratch, dma, *([] if last else [dma((PARTS, 2))])],
                tile_total * 2**22, "local", {6: 2} if last else {7: 3},
            )(
                lists, counts, field, mate, near, *([] if last else [source_factor]),
                pinned(tail), streamed(out),
            )
            source = None if last else source[0]
        near_operands = (lists, counts, pinned(tiles), outer)
        if step == ITERS - 1:
            acc = call(
                last_others_kernel, acc_type, [SMEM, SMEM, VMEM, VMEM, VMEM], VMEM,
                [], tile_total * 2**22, "others", {4: 0},
            )(*near_operands, pinned(acc))
            return call(
                lambda *refs, step=step: last_kernel(step, *refs),
                out_type, [SMEM, SMEM, VMEM, ANY, VMEM, ANY], ANY,
                [picked_type, half_type, done_type, dma((PARTS, 2)), dma((PARTS,))],
                far_flops, "last", {5: 0},
            )(turned_src, far_count, received, target_factor, pinned(acc), streamed(out))
        acc, x = call(
            others_kernel, (acc_type, x_type), [SMEM, SMEM, VMEM, VMEM, VMEM, VMEM], (VMEM, VMEM),
            [], tile_total * 2**22, "others", {5: 0},
        )(*near_operands, pinned(source), pinned(acc))
        width = panels // PARTS * KEPT
        field, send, out, tail = call(
            lambda *refs, step=step: far_kernel(step, *refs),
            (field_type, send_type, out_type, pltpu.VMEM((excite, width), F32)),
            [SMEM, SMEM, SMEM, VMEM, ANY, ANY, VMEM, VMEM, ANY], (VMEM, ANY, ANY, VMEM),
            [
                pltpu.VMEM(gram_shape, BF16), picked_type, picked_type, half_type,
                pltpu.VMEM((excite, panels - width), F32),
                dma((PARTS, 2)), dma((slots,)), dma, dma((PARTS - KEPT,)),
            ],
            far_flops, "far", {8: 2},
        )(
            turned_src, far_count, dest, received, target_factor, streamed(gram), pinned(acc), pinned(x),
            streamed(out),
        )


def solution(mesh):
    in_specs = (
        P(None, "panels"),
        P("panels", None, None, None),
        P("panels", None),
        P("panels"),
        P(),
        P(),
        P(None, None, "panels"),
        P(None, None, "panels"),
    )
    out_specs = P(None, None, "panels")
    return jax.shard_map(shards, mesh=mesh, in_specs=in_specs, out_specs=out_specs, check_vma=False)
```

```python
import jax
import jax.numpy as jnp
from jax import lax
from jax.experimental import pallas as pl
from jax.experimental.pallas import tpu as pltpu
from jax.sharding import PartitionSpec as P

ITERS = 5
BATCH = 8
PARTS = 4
KEPT = 2
F32 = jnp.float32
BF16 = jnp.bfloat16
NT = (((1,), (1,)), ((), ()))
VMEM = pl.BlockSpec(memory_space=pltpu.VMEM)
SMEM = pl.BlockSpec(memory_space=pltpu.SMEM)
ANY = pl.BlockSpec(memory_space=pl.ANY)
LIMIT = 24 * 2**20


def nt(a, b):
    return lax.dot_general(a, b, NT, preferred_element_type=F32)


def pinned(x):
    return pltpu.with_memory_space_constraint(x, pltpu.VMEM)


def streamed(x):
    return pltpu.with_memory_space_constraint(x, pltpu.HBM)


def params():
    return pltpu.CompilerParams(vmem_limit_bytes=LIMIT)


def cost(flops, touched):
    return pl.CostEstimate(flops=flops, bytes_accessed=touched, transcendentals=0)


def place(dest, x, send, sem):
    slots = x.shape[0] // 16

    def copy(q):
        return pltpu.make_async_copy(x.at[pl.ds(16 * q, 16)], send.at[dest[0, q]], sem.at[q])

    for act in ("start", "wait"):
        for q in range(slots):

            @pl.when(dest[0, q] >= 0)
            def _():
                getattr(copy(q), act)()

        if act == "start":
            yield
    yield


def project(source, accs, i, leaf):
    out = []
    for h in range(2):
        part = source[h, :, :, 256 * i : 256 * i + 256]
        term = nt(part.reshape(-1, 256), leaf)
        out.append(term if accs is None else accs[h] + term)
    return out


def half_copy(factor, wide, sems, c, h):
    width = wide.shape[3] // sems.shape[0]
    cols = pl.ds(c * width, width)
    return pltpu.make_async_copy(factor.at[:, pl.ds(16 * h, 16), cols], wide.at[h, :, :, cols], sems.at[c, h])


def start_halves(factor, wide, sems):
    for c in range(sems.shape[0]):
        for h in range(2):
            half_copy(factor, wide, sems, c, h).start()


def wait_halves(factor, wide, sems, c):
    for h in range(2):
        half_copy(factor, wide, sems, c, h).wait()


def destinations(far_src, far_count):
    slots, rows = far_src.shape
    live = lax.broadcasted_iota(jnp.int32, (slots, rows), 0) < far_count
    hits = jnp.where((far_src == lax.axis_index("panels")) & live, 1.0, 0.0)
    has = jnp.max(hits, axis=0, keepdims=True)
    first = lax.broadcasted_iota(jnp.int32, (rows, rows), 0)
    second = lax.broadcasted_iota(jnp.int32, (rows, rows), 1)
    wide = jnp.broadcast_to(has, (8, rows))
    rank = jnp.dot(wide, jnp.where(first < second, 1.0, 0.0), preferred_element_type=F32)[:1]
    match = jnp.where((rank == first.astype(F32)) & (has > 0.5), 1.0, 0.0)
    order = lax.broadcasted_iota(jnp.int32, (8, rows), 1).astype(F32) + 1.0
    return nt(order, match)[:1].astype(jnp.int32) - 1


def first_kernel(
    far_src, far_count, field_in, factor, send, field, dest,
    source, x, src_here, count_here, dest_here, sems, psem, fsem, lsems,
):
    plan = [
        pltpu.make_async_copy(far_src, src_here, lsems.at[0]),
        pltpu.make_async_copy(far_count, count_here.at[0], lsems.at[1]),
    ]
    for copy in plan:
        copy.start()
    brought = pltpu.make_async_copy(field_in, field, fsem)
    brought.start()
    start_halves(factor, source, sems)
    for copy in plan:
        copy.wait()
    dest_here[...] = destinations(src_here[...], count_here[...])
    placed = pltpu.make_async_copy(dest_here, dest, lsems.at[2])
    placed.start()
    brought.wait()
    parts = sems.shape[0]
    per = field.shape[1] // 256 // parts
    accs = None
    for c in range(parts):
        wait_halves(factor, source, sems, c)
        for i in range(c * per, c * per + per):
            accs = project(source, accs, i, field[:, 256 * i : 256 * i + 256])
    x[...] = jnp.concatenate(accs, axis=1).astype(BF16)
    placed.wait()
    for _ in place(dest, x, send, psem):
        pass


def fetch_list(lists, groups, which, base, near, tiles, sem_of):
    def body(g, carry):
        for b in range(BATCH):
            e = g * BATCH + b
            pltpu.make_async_copy(near.at[lists[which, 0, e]], tiles.at[base + e], sem_of(g)).start()
        return carry

    lax.fori_loop(0, groups, body, 0)


def arrived(near, tiles, sem, at):
    pltpu.make_async_copy(near.at[pl.ds(0, BATCH)], tiles.at[pl.ds(at, BATCH)], sem).wait()


def run_list(lists, groups, which, base, tiles, field, acc, ready=None):
    def body(g, carry):
        if ready is not None:
            ready(g)
        found = []
        for b in range(BATCH):
            e = g * BATCH + b
            at = pl.multiple_of(lists[which, 1, e], 256)
            found.append(nt(field[:, pl.ds(at, 256)], tiles[base + e]))
        for b in range(BATCH):
            e = g * BATCH + b
            acc[lists[which, 2, e]] += found[b]
        return carry

    lax.fori_loop(0, groups, body, 0)


def own_part(lists, counts, field, mate, near, acc, others, tiles, sems, osem, both, bsems, between=None):
    panels = field.shape[1]
    brought = [
        pltpu.make_async_copy(part, both.at[:, pl.ds(panels * k, panels)], bsems.at[k])
        for k, part in enumerate((field, mate))
    ]
    for copy in brought:
        copy.start()
    fetch_list(lists, counts[0], 0, 0, near, tiles, lambda g: sems.at[g])
    fetch_list(lists, counts[1], 1, 0, near, others, lambda g: osem)
    if between is not None:
        between()
    acc[...] = jnp.zeros_like(acc)
    for copy in brought:
        copy.wait()

    def ready(g):
        arrived(near, tiles, sems.at[g], g * BATCH)

    run_list(lists, counts[0], 0, 0, tiles, both, acc, ready)

    def body(g, carry):
        arrived(near, others, osem, g * BATCH)
        return carry

    lax.fori_loop(0, counts[1], body, 0)


def setup_kernel(
    offset, count, field, mate, near, source_factor, target_factor,
    acc, others, source, gram, lists, counts, out, tiles, sems, osem, mate_here, msem, target, ssems, tsems,
):
    start_halves(source_factor, source, ssems)
    start_halves(target_factor, target, tsems)
    leaves = count.shape[0]
    slots = near.shape[0] // leaves
    odd = lax.axis_index("panels") % 2

    def leaf_body(i, filled):
        def slot_body(j, filled):
            at_leaf = i + offset[j, i]
            outside = (at_leaf < 0) | (at_leaf >= leaves)
            off_chip = jnp.where(odd == 1, at_leaf >= leaves, at_leaf < 0)
            which = jnp.where(off_chip, 1, 0)
            inside = jnp.where(at_leaf < 0, at_leaf + leaves, jnp.where(at_leaf >= leaves, at_leaf - leaves, at_leaf))
            at = jnp.where(off_chip, filled[1], filled[0])
            lists[which, 0, at] = i * slots + j
            lists[which, 1, at] = 256 * (inside + jnp.where(outside & ~off_chip, leaves, 0))
            lists[which, 2, at] = i
            return filled[0] + 1 - which, filled[1] + which

        return lax.fori_loop(0, count[i], slot_body, filled)

    zero = jnp.int32(0)
    filled = lax.fori_loop(0, leaves, leaf_body, (zero, zero))
    for w in range(2):
        groups = (filled[w] + BATCH - 1) // BATCH

        def fill(e, carry, w=w):
            lists[w, 0, e] = 0
            lists[w, 1, e] = 0
            lists[w, 2, e] = leaves
            return carry

        lax.fori_loop(filled[w], groups * BATCH, fill, 0)
        counts[w] = groups

    def couple():
        panels = source.shape[3]
        for c in range(ssems.shape[0]):
            wait_halves(source_factor, source, ssems, c)
            wait_halves(target_factor, target, tsems, c)
        for h in range(2):
            for g in range(2):
                gram[h, g] = nt(source[h].reshape(-1, panels), target[g].reshape(-1, panels)).astype(BF16)

    own_part(lists, counts, field, mate, near, acc, others, tiles, sems, osem, mate_here, msem, couple)


def store_tail(step, tail, out, sem):
    width = tail.shape[1]
    return pltpu.make_async_copy(tail, out.at[step - 1, :, pl.ds(out.shape[2] - width, width)], sem)


def local_kernel(
    step, lists, counts, field, mate, near, factor, tail, _, acc, others, source, out,
    tiles, sems, osem, both, bsems, sem, ssems,
):
    copy = store_tail(step, tail, out, sem)
    copy.start()
    own_part(
        lists, counts, field, mate, near, acc, others, tiles, sems, osem, both, bsems,
        lambda: start_halves(factor, source, ssems),
    )
    for c in range(ssems.shape[0]):
        wait_halves(factor, source, ssems, c)
    copy.wait()


def last_local_kernel(step, lists, counts, field, mate, near, tail, _, acc, others, out, *scratch):
    *scratch, sem = scratch
    copy = store_tail(step, tail, out, sem)
    copy.start()
    own_part(lists, counts, field, mate, near, acc, others, *scratch)
    copy.wait()


def others_part(lists, counts, tiles, outer, acc):
    run_list(lists, counts[1], 1, 0, tiles, outer, acc)


def others_kernel(lists, counts, tiles, outer, source, _, acc, x):
    others_part(lists, counts, tiles, outer, acc)
    accs = None
    for i in range(acc.shape[0] - 1):
        accs = project(source, accs, i, acc[i].astype(BF16))
    x[...] = jnp.concatenate(accs, axis=1)


def last_others_kernel(lists, counts, tiles, outer, _, acc):
    others_part(lists, counts, tiles, outer, acc)


def pick(far_src, far_count, received, picked):
    own = lax.axis_index("panels")
    live = far_count[own]
    for k in range(picked.shape[0] // 16):
        block = received[far_src[k, own]]
        picked[16 * k : 16 * k + 16] = jnp.where(k < live, block, jnp.zeros_like(block))


def expand(target_factor, acc, picked, wide, tsems, use, passed):
    turned = picked[...].astype(F32).T.astype(BF16)
    excite = turned.shape[0] // 2
    parts = tsems.shape[0]
    per = wide.shape[3] // 256 // parts
    for c in range(parts):
        wait_halves(target_factor, wide, tsems, c)
        for i in range(c * per, c * per + per):
            cols = slice(256 * i, 256 * i + 256)
            value = acc[i]
            for h in range(2):
                value += jnp.dot(
                    turned[excite * h : excite * h + excite],
                    wide[h, :, :, cols].reshape(-1, 256),
                    preferred_element_type=F32,
                )
            use(cols, value)
        passed(c)


def far_kernel(
    step, far_src, far_count, dest, received, target_factor, gram_in, acc, x, _, field, send, out, tail,
    gram, picked, ready, wide, done, tsems, psems, gsem, osems,
):
    brought = pltpu.make_async_copy(gram_in, gram, gsem)
    brought.start()
    start_halves(target_factor, wide, tsems)
    pick(far_src, far_count, received, picked)
    excite = picked.shape[1] // 2
    brought.wait()
    parts = []
    for h in range(2):
        part = x[:, excite * h : excite * h + excite]
        for g in range(2):
            part += jnp.dot(
                gram[h, g], picked[:, excite * g : excite * g + excite], preferred_element_type=F32
            )
        parts.append(part)
    ready[...] = jnp.concatenate(parts, axis=1).astype(BF16)
    placed = place(dest, ready, send, psems)
    next(placed)

    kept = done.shape[1]

    def use(cols, value):
        if cols.start < kept:
            done[:, cols] = value
        else:
            tail[:, cols.start - kept : cols.stop - kept] = value
        field[:, cols] = value.astype(BF16)

    copies = []

    def passed(c):
        if c < osems.shape[0]:
            store_part(step, c, done, out, osems, copies)

    expand(target_factor, acc, picked, wide, tsems, use, passed)
    next(placed)
    for copy in copies:
        copy.wait()


def store_part(step, c, done, out, osems, copies):
    width = done.shape[1] // osems.shape[0]
    cols = pl.ds(width * c, width)
    copies.append(pltpu.make_async_copy(done.at[:, cols], out.at[step, :, cols], osems.at[c]))
    copies[-1].start()


def last_kernel(step, far_src, far_count, received, target_factor, acc, _, out, picked, wide, done, tsems, osems):
    start_halves(target_factor, wide, tsems)
    pick(far_src, far_count, received, picked)
    copies = []

    def use(cols, value):
        done[:, cols] = value

    expand(target_factor, acc, picked, wide, tsems, use, lambda c: store_part(step, c, done, out, osems, copies))
    for copy in copies:
        copy.wait()


def shards(
    excitation, near_tiles, near_offset, near_count, far_src, far_count, source_factor, target_factor
):
    excite, panels = excitation.shape
    leaves, near_slots, leaf = near_tiles.shape[:3]
    rows, slots = far_src.shape
    rank = source_factor.shape[1]
    count = lax.axis_size("panels")

    tile_total = leaves * near_slots
    near = streamed(near_tiles.reshape(tile_total, leaf, leaf))
    source_factor, target_factor = streamed(source_factor), streamed(target_factor)
    entries = tile_total + BATCH
    half = slots * rank // 2
    send_type = pltpu.HBM((rows, rank // 2, 2 * excite), BF16)
    field_type = jax.ShapeDtypeStruct((excite, panels), BF16)
    acc_type = pltpu.VMEM((leaves + 1, excite, leaf), F32)
    out_type = pltpu.HBM((ITERS, excite, panels), F32)
    tiles_type = pltpu.VMEM((entries, leaf, leaf), BF16)
    half_type = pltpu.VMEM((2, slots, rank // 2, panels), BF16)
    done_type = pltpu.VMEM((excite, panels), F32)
    picked_type = pltpu.VMEM((half, 2 * excite), BF16)
    x_type = pltpu.VMEM((half, 2 * excite), F32)
    gram_shape = (2, 2, half, half)
    dma = pltpu.SemaphoreType.DMA
    groups = entries // BATCH
    far_flops = 2 * slots * rank * panels * excite

    def call(kernel, out_shape, in_specs, out_specs, scratch, flops, name, aliases=None):
        return pl.pallas_call(
            kernel,
            out_shape=out_shape,
            in_specs=in_specs,
            out_specs=out_specs,
            scratch_shapes=scratch,
            input_output_aliases=aliases or {},
            compiler_params=params(),
            cost_estimate=cost(flops, 2**22),
            name=name,
        )

    outward = [(i, (i + 2 * (i % 2) - 1) % count) for i in range(count)]
    inward = [(i, i + 1 - 2 * (i % 2)) for i in range(count)]
    field = send = lists = counts = out = gram = None
    turned_src = far_src.T
    for step in range(ITERS):
        if step == 0:
            row_type = jax.ShapeDtypeStruct((1, rows), jnp.int32)
            send, field, dest = call(
                first_kernel, (send_type, field_type, row_type), [ANY, ANY, ANY, ANY], (ANY, VMEM, SMEM),
                [
                    half_type, picked_type, pltpu.VMEM((slots, rows), jnp.int32),
                    pltpu.VMEM((1, rows), jnp.int32), pltpu.VMEM((1, rows), jnp.int32),
                    dma((PARTS, 2)), dma((slots,)), dma, dma((3,)),
                ],
                far_flops, "first",
            )(streamed(turned_src), streamed(far_count), streamed(excitation), source_factor)
        outer = lax.ppermute(field, "panels", outward)
        mate = lax.ppermute(field, "panels", inward)
        received = lax.all_to_all(send, "panels", split_axis=0, concat_axis=0, tiled=True)
        own_scratch = [tiles_type, dma((groups,)), dma, pltpu.VMEM((excite, 2 * panels), BF16), dma((2,))]
        if step == 0:
            acc, tiles, source, gram, lists, counts, out = call(
                setup_kernel,
                (
                    acc_type, tiles_type, half_type, pltpu.HBM(gram_shape, BF16),
                    jax.ShapeDtypeStruct((2, 3, entries), jnp.int32),
                    jax.ShapeDtypeStruct((2,), jnp.int32),
                    out_type,
                ),
                [SMEM, SMEM, ANY, ANY, ANY, ANY, ANY], (VMEM, VMEM, VMEM, VMEM, SMEM, SMEM, ANY),
                [*own_scratch, half_type, dma((PARTS, 2)), dma((PARTS, 2))],
                tile_total * 2**22, "setup",
            )(near_offset.T, near_count, field, mate, near, source_factor, target_factor)
        else:
            last = step == ITERS - 1
            acc, tiles, *source, out = call(
                lambda *refs, step=step, last=last: (last_local_kernel if last else local_kernel)(step, *refs),
                (acc_type, tiles_type, *([] if last else [half_type]), out_type),
                [SMEM, SMEM, ANY, ANY, ANY, *([] if last else [ANY]), VMEM, ANY],
                (VMEM, VMEM, *([] if last else [VMEM]), ANY),
                [*own_scratch, dma, *([] if last else [dma((PARTS, 2))])],
                tile_total * 2**22, "local", {6: 2} if last else {7: 3},
            )(
                lists, counts, field, mate, near, *([] if last else [source_factor]),
                pinned(tail), streamed(out),
            )
            source = None if last else source[0]
        near_operands = (lists, counts, pinned(tiles), outer)
        if step == ITERS - 1:
            acc = call(
                last_others_kernel, acc_type, [SMEM, SMEM, VMEM, VMEM, VMEM], VMEM,
                [], tile_total * 2**22, "others", {4: 0},
            )(*near_operands, pinned(acc))
            return call(
                lambda *refs, step=step: last_kernel(step, *refs),
                out_type, [SMEM, SMEM, VMEM, ANY, VMEM, ANY], ANY,
                [picked_type, half_type, done_type, dma((PARTS, 2)), dma((PARTS,))],
                far_flops, "last", {5: 0},
            )(turned_src, far_count, received, target_factor, pinned(acc), streamed(out))
        acc, x = call(
            others_kernel, (acc_type, x_type), [SMEM, SMEM, VMEM, VMEM, VMEM, VMEM], (VMEM, VMEM),
            [], tile_total * 2**22, "others", {5: 0},
        )(*near_operands, pinned(source), pinned(acc))
        width = panels // PARTS * KEPT
        field, send, out, tail = call(
            lambda *refs, step=step: far_kernel(step, *refs),
            (field_type, send_type, out_type, pltpu.VMEM((excite, width), F32)),
            [SMEM, SMEM, SMEM, VMEM, ANY, ANY, VMEM, VMEM, ANY], (VMEM, ANY, ANY, VMEM),
            [
                pltpu.VMEM(gram_shape, BF16), picked_type, picked_type, half_type,
                pltpu.VMEM((excite, panels - width), F32),
                dma((PARTS, 2)), dma((slots,)), dma, dma((PARTS - KEPT,)),
            ],
            far_flops, "far", {8: 2},
        )(
            turned_src, far_count, dest, received, target_factor, streamed(gram), pinned(acc), pinned(x),
            streamed(out),
        )


def solution(mesh):
    in_specs = (
        P(None, "panels"),
        P("panels", None, None, None),
        P("panels", None),
        P("panels"),
        P(),
        P(),
        P(None, None, "panels"),
        P(None, None, "panels"),
    )
    out_specs = P(None, None, "panels")
    return jax.shard_map(shards, mesh=mesh, in_specs=in_specs, out_specs=out_specs, check_vma=False)
```

```python
import jax
import jax.numpy as jnp
from jax import lax
from jax.experimental import pallas as pl
from jax.experimental.pallas import tpu as pltpu
from jax.sharding import PartitionSpec as P

ITERS = 5
BATCH = 8
PARTS = 4
KEPT = 2
F32 = jnp.float32
BF16 = jnp.bfloat16
NT = (((1,), (1,)), ((), ()))
VMEM = pl.BlockSpec(memory_space=pltpu.VMEM)
SMEM = pl.BlockSpec(memory_space=pltpu.SMEM)
ANY = pl.BlockSpec(memory_space=pl.ANY)
LIMIT = 24 * 2**20


def nt(a, b):
    return lax.dot_general(a, b, NT, preferred_element_type=F32)


def pinned(x):
    return pltpu.with_memory_space_constraint(x, pltpu.VMEM)


def streamed(x):
    return pltpu.with_memory_space_constraint(x, pltpu.HBM)


def params():
    return pltpu.CompilerParams(vmem_limit_bytes=LIMIT)


def cost(flops, touched):
    return pl.CostEstimate(flops=flops, bytes_accessed=touched, transcendentals=0)


def place(dest, x, send, sem):
    slots = x.shape[0] // 16

    def copy(q):
        return pltpu.make_async_copy(x.at[pl.ds(16 * q, 16)], send.at[dest[0, q]], sem.at[q])

    for act in ("start", "wait"):
        for q in range(slots):

            @pl.when(dest[0, q] >= 0)
            def _():
                getattr(copy(q), act)()

        if act == "start":
            yield
    yield


def project(source, accs, i, leaf):
    out = []
    for h in range(2):
        part = source[h, :, :, 256 * i : 256 * i + 256]
        term = nt(part.reshape(-1, 256), leaf)
        out.append(term if accs is None else accs[h] + term)
    return out


def half_copy(factor, wide, sems, c, h):
    width = wide.shape[3] // sems.shape[0]
    cols = pl.ds(c * width, width)
    return pltpu.make_async_copy(factor.at[:, pl.ds(16 * h, 16), cols], wide.at[h, :, :, cols], sems.at[c, h])


def start_halves(factor, wide, sems):
    for c in range(sems.shape[0]):
        for h in range(2):
            half_copy(factor, wide, sems, c, h).start()


def wait_halves(factor, wide, sems, c):
    for h in range(2):
        half_copy(factor, wide, sems, c, h).wait()


def destinations(far_src, far_count):
    slots, rows = far_src.shape
    live = lax.broadcasted_iota(jnp.int32, (slots, rows), 0) < far_count
    hits = jnp.where((far_src == lax.axis_index("panels")) & live, 1.0, 0.0)
    has = jnp.max(hits, axis=0, keepdims=True)
    first = lax.broadcasted_iota(jnp.int32, (rows, rows), 0)
    second = lax.broadcasted_iota(jnp.int32, (rows, rows), 1)
    wide = jnp.broadcast_to(has, (8, rows))
    rank = jnp.dot(wide, jnp.where(first < second, 1.0, 0.0), preferred_element_type=F32)[:1]
    match = jnp.where((rank == first.astype(F32)) & (has > 0.5), 1.0, 0.0)
    order = lax.broadcasted_iota(jnp.int32, (8, rows), 1).astype(F32) + 1.0
    return nt(order, match)[:1].astype(jnp.int32) - 1


def first_kernel(
    far_src, far_count, field_in, factor, send, field, dest,
    source, x, src_here, count_here, dest_here, sems, psem, fsem, lsems,
):
    plan = [
        pltpu.make_async_copy(far_src, src_here, lsems.at[0]),
        pltpu.make_async_copy(far_count, count_here.at[0], lsems.at[1]),
    ]
    for copy in plan:
        copy.start()
    brought = pltpu.make_async_copy(field_in, field, fsem)
    brought.start()
    start_halves(factor, source, sems)
    for copy in plan:
        copy.wait()
    dest_here[...] = destinations(src_here[...], count_here[...])
    placed = pltpu.make_async_copy(dest_here, dest, lsems.at[2])
    placed.start()
    brought.wait()
    parts = sems.shape[0]
    per = field.shape[1] // 256 // parts
    accs = None
    for c in range(parts):
        wait_halves(factor, source, sems, c)
        for i in range(c * per, c * per + per):
            accs = project(source, accs, i, field[:, 256 * i : 256 * i + 256])
    x[...] = jnp.concatenate(accs, axis=1).astype(BF16)
    placed.wait()
    for _ in place(dest, x, send, psem):
        pass


def fetch_list(lists, groups, which, base, near, tiles, sem_of):
    def body(g, carry):
        for b in range(BATCH):
            e = g * BATCH + b
            pltpu.make_async_copy(near.at[lists[which, 0, e]], tiles.at[base + e], sem_of(g)).start()
        return carry

    lax.fori_loop(0, groups, body, 0)


def arrived(near, tiles, sem, at):
    pltpu.make_async_copy(near.at[pl.ds(0, BATCH)], tiles.at[pl.ds(at, BATCH)], sem).wait()


def run_list(lists, groups, which, base, tiles, field, acc, ready=None):
    def body(g, carry):
        if ready is not None:
            ready(g)
        found = []
        for b in range(BATCH):
            e = g * BATCH + b
            at = pl.multiple_of(lists[which, 1, e], 256)
            found.append(nt(field[:, pl.ds(at, 256)], tiles[base + e]))
        for b in range(BATCH):
            e = g * BATCH + b
            acc[lists[which, 2, e]] += found[b]
        return carry

    lax.fori_loop(0, groups, body, 0)


def own_part(lists, counts, field, mate, near, acc, others, tiles, sems, osem, both, bsems, between=None):
    panels = field.shape[1]
    brought = [
        pltpu.make_async_copy(part, both.at[:, pl.ds(panels * k, panels)], bsems.at[k])
        for k, part in enumerate((field, mate))
    ]
    for copy in brought:
        copy.start()
    fetch_list(lists, counts[0], 0, 0, near, tiles, lambda g: sems.at[g])
    fetch_list(lists, counts[1], 1, 0, near, others, lambda g: osem)
    if between is not None:
        between()
    acc[...] = jnp.zeros_like(acc)
    for copy in brought:
        copy.wait()

    def ready(g):
        arrived(near, tiles, sems.at[g], g * BATCH)

    run_list(lists, counts[0], 0, 0, tiles, both, acc, ready)

    def body(g, carry):
        arrived(near, others, osem, g * BATCH)
        return carry

    lax.fori_loop(0, counts[1], body, 0)


def setup_kernel(
    offset, count, field, mate, near, source_factor, target_factor,
    acc, others, source, gram, lists, counts, out, tiles, sems, osem, mate_here, msem, target, ssems, tsems,
):
    start_halves(source_factor, source, ssems)
    start_halves(target_factor, target, tsems)
    leaves = count.shape[0]
    slots = near.shape[0] // leaves
    odd = lax.axis_index("panels") % 2

    def leaf_body(i, filled):
        def slot_body(j, filled):
            at_leaf = i + offset[j, i]
            outside = (at_leaf < 0) | (at_leaf >= leaves)
            off_chip = jnp.where(odd == 1, at_leaf >= leaves, at_leaf < 0)
            which = jnp.where(off_chip, 1, 0)
            inside = jnp.where(at_leaf < 0, at_leaf + leaves, jnp.where(at_leaf >= leaves, at_leaf - leaves, at_leaf))
            at = jnp.where(off_chip, filled[1], filled[0])
            lists[which, 0, at] = i * slots + j
            lists[which, 1, at] = 256 * (inside + jnp.where(outside & ~off_chip, leaves, 0))
            lists[which, 2, at] = i
            return filled[0] + 1 - which, filled[1] + which

        return lax.fori_loop(0, count[i], slot_body, filled)

    zero = jnp.int32(0)
    filled = lax.fori_loop(0, leaves, leaf_body, (zero, zero))
    for w in range(2):
        groups = (filled[w] + BATCH - 1) // BATCH

        def fill(e, carry, w=w):
            lists[w, 0, e] = 0
            lists[w, 1, e] = 0
            lists[w, 2, e] = leaves
            return carry

        lax.fori_loop(filled[w], groups * BATCH, fill, 0)
        counts[w] = groups

    def couple():
        panels = source.shape[3]
        for c in range(ssems.shape[0]):
            wait_halves(source_factor, source, ssems, c)
            wait_halves(target_factor, target, tsems, c)
        for g in range(2):
            both_halves = nt(source[...].reshape(-1, panels), target[g].reshape(-1, panels)).astype(BF16)
            for h in range(2):
                gram[h, g] = both_halves[256 * h : 256 * h + 256]

    own_part(lists, counts, field, mate, near, acc, others, tiles, sems, osem, mate_here, msem, couple)


def store_tail(step, tail, out, sem):
    width = tail.shape[1]
    return pltpu.make_async_copy(tail, out.at[step - 1, :, pl.ds(out.shape[2] - width, width)], sem)


def local_kernel(
    step, lists, counts, field, mate, near, factor, tail, _, acc, others, source, out,
    tiles, sems, osem, both, bsems, sem, ssems,
):
    copy = store_tail(step, tail, out, sem)
    copy.start()
    own_part(
        lists, counts, field, mate, near, acc, others, tiles, sems, osem, both, bsems,
        lambda: start_halves(factor, source, ssems),
    )
    for c in range(ssems.shape[0]):
        wait_halves(factor, source, ssems, c)
    copy.wait()


def last_local_kernel(step, lists, counts, field, mate, near, tail, _, acc, others, out, *scratch):
    *scratch, sem = scratch
    copy = store_tail(step, tail, out, sem)
    copy.start()
    own_part(lists, counts, field, mate, near, acc, others, *scratch)
    copy.wait()


def others_part(lists, counts, tiles, outer, acc):
    run_list(lists, counts[1], 1, 0, tiles, outer, acc)


def others_kernel(lists, counts, tiles, outer, source, _, acc, x):
    others_part(lists, counts, tiles, outer, acc)
    accs = None
    for i in range(acc.shape[0] - 1):
        accs = project(source, accs, i, acc[i].astype(BF16))
    x[...] = jnp.concatenate(accs, axis=1)


def last_others_kernel(lists, counts, tiles, outer, _, acc):
    others_part(lists, counts, tiles, outer, acc)


def pick(far_src, far_count, received, picked):
    own = lax.axis_index("panels")
    live = far_count[own]
    for k in range(picked.shape[0] // 16):
        block = received[far_src[k, own]]
        picked[16 * k : 16 * k + 16] = jnp.where(k < live, block, jnp.zeros_like(block))


def expand(target_factor, acc, picked, wide, tsems, use, passed):
    turned = picked[...].astype(F32).T.astype(BF16)
    excite = turned.shape[0] // 2
    parts = tsems.shape[0]
    per = wide.shape[3] // 256 // parts
    for c in range(parts):
        wait_halves(target_factor, wide, tsems, c)
        for i in range(c * per, c * per + per):
            cols = slice(256 * i, 256 * i + 256)
            value = acc[i]
            for h in range(2):
                value += jnp.dot(
                    turned[excite * h : excite * h + excite],
                    wide[h, :, :, cols].reshape(-1, 256),
                    preferred_element_type=F32,
                )
            use(cols, value)
        passed(c)


def far_kernel(
    step, far_src, far_count, dest, received, target_factor, gram_in, acc, x, _, field, send, out, tail,
    gram, picked, ready, wide, done, tsems, psems, gsem, osems,
):
    brought = pltpu.make_async_copy(gram_in, gram, gsem)
    brought.start()
    start_halves(target_factor, wide, tsems)
    pick(far_src, far_count, received, picked)
    excite = picked.shape[1] // 2
    brought.wait()
    parts = []
    for h in range(2):
        part = x[:, excite * h : excite * h + excite]
        for g in range(2):
            part += jnp.dot(
                gram[h, g], picked[:, excite * g : excite * g + excite], preferred_element_type=F32
            )
        parts.append(part)
    ready[...] = jnp.concatenate(parts, axis=1).astype(BF16)
    placed = place(dest, ready, send, psems)
    next(placed)

    kept = done.shape[1]

    def use(cols, value):
        if cols.start < kept:
            done[:, cols] = value
        else:
            tail[:, cols.start - kept : cols.stop - kept] = value
        field[:, cols] = value.astype(BF16)

    copies = []

    def passed(c):
        if c < osems.shape[0]:
            store_part(step, c, done, out, osems, copies)

    expand(target_factor, acc, picked, wide, tsems, use, passed)
    next(placed)
    for copy in copies:
        copy.wait()


def store_part(step, c, done, out, osems, copies):
    width = done.shape[1] // osems.shape[0]
    cols = pl.ds(width * c, width)
    copies.append(pltpu.make_async_copy(done.at[:, cols], out.at[step, :, cols], osems.at[c]))
    copies[-1].start()


def last_kernel(step, far_src, far_count, received, target_factor, acc, _, out, picked, wide, done, tsems, osems):
    start_halves(target_factor, wide, tsems)
    pick(far_src, far_count, received, picked)
    copies = []

    def use(cols, value):
        done[:, cols] = value

    expand(target_factor, acc, picked, wide, tsems, use, lambda c: store_part(step, c, done, out, osems, copies))
    for copy in copies:
        copy.wait()


def shards(
    excitation, near_tiles, near_offset, near_count, far_src, far_count, source_factor, target_factor
):
    excite, panels = excitation.shape
    leaves, near_slots, leaf = near_tiles.shape[:3]
    rows, slots = far_src.shape
    rank = source_factor.shape[1]
    count = lax.axis_size("panels")

    tile_total = leaves * near_slots
    near = streamed(near_tiles.reshape(tile_total, leaf, leaf))
    source_factor, target_factor = streamed(source_factor), streamed(target_factor)
    entries = tile_total + BATCH
    half = slots * rank // 2
    send_type = pltpu.HBM((rows, rank // 2, 2 * excite), BF16)
    field_type = jax.ShapeDtypeStruct((excite, panels), BF16)
    acc_type = pltpu.VMEM((leaves + 1, excite, leaf), F32)
    out_type = pltpu.HBM((ITERS, excite, panels), F32)
    tiles_type = pltpu.VMEM((entries, leaf, leaf), BF16)
    half_type = pltpu.VMEM((2, slots, rank // 2, panels), BF16)
    done_type = pltpu.VMEM((excite, panels), F32)
    picked_type = pltpu.VMEM((half, 2 * excite), BF16)
    x_type = pltpu.VMEM((half, 2 * excite), F32)
    gram_shape = (2, 2, half, half)
    dma = pltpu.SemaphoreType.DMA
    groups = entries // BATCH
    far_flops = 2 * slots * rank * panels * excite

    def call(kernel, out_shape, in_specs, out_specs, scratch, flops, name, aliases=None):
        return pl.pallas_call(
            kernel,
            out_shape=out_shape,
            in_specs=in_specs,
            out_specs=out_specs,
            scratch_shapes=scratch,
            input_output_aliases=aliases or {},
            compiler_params=params(),
            cost_estimate=cost(flops, 2**22),
            name=name,
        )

    outward = [(i, (i + 2 * (i % 2) - 1) % count) for i in range(count)]
    inward = [(i, i + 1 - 2 * (i % 2)) for i in range(count)]
    field = send = lists = counts = out = gram = None
    turned_src = far_src.T
    for step in range(ITERS):
        if step == 0:
            row_type = jax.ShapeDtypeStruct((1, rows), jnp.int32)
            send, field, dest = call(
                first_kernel, (send_type, field_type, row_type), [ANY, ANY, ANY, ANY], (ANY, VMEM, SMEM),
                [
                    half_type, picked_type, pltpu.VMEM((slots, rows), jnp.int32),
                    pltpu.VMEM((1, rows), jnp.int32), pltpu.VMEM((1, rows), jnp.int32),
                    dma((PARTS, 2)), dma((slots,)), dma, dma((3,)),
                ],
                far_flops, "first",
            )(streamed(turned_src), streamed(far_count), streamed(excitation), source_factor)
        outer = lax.ppermute(field, "panels", outward)
        mate = lax.ppermute(field, "panels", inward)
        received = lax.all_to_all(send, "panels", split_axis=0, concat_axis=0, tiled=True)
        own_scratch = [tiles_type, dma((groups,)), dma, pltpu.VMEM((excite, 2 * panels), BF16), dma((2,))]
        if step == 0:
            acc, tiles, source, gram, lists, counts, out = call(
                setup_kernel,
                (
                    acc_type, tiles_type, half_type, pltpu.HBM(gram_shape, BF16),
                    jax.ShapeDtypeStruct((2, 3, entries), jnp.int32),
                    jax.ShapeDtypeStruct((2,), jnp.int32),
                    out_type,
                ),
                [SMEM, SMEM, ANY, ANY, ANY, ANY, ANY], (VMEM, VMEM, VMEM, VMEM, SMEM, SMEM, ANY),
                [*own_scratch, half_type, dma((PARTS, 2)), dma((PARTS, 2))],
                tile_total * 2**22, "setup",
            )(near_offset.T, near_count, field, mate, near, source_factor, target_factor)
        else:
            last = step == ITERS - 1
            acc, tiles, *source, out = call(
                lambda *refs, step=step, last=last: (last_local_kernel if last else local_kernel)(step, *refs),
                (acc_type, tiles_type, *([] if last else [half_type]), out_type),
                [SMEM, SMEM, ANY, ANY, ANY, *([] if last else [ANY]), VMEM, ANY],
                (VMEM, VMEM, *([] if last else [VMEM]), ANY),
                [*own_scratch, dma, *([] if last else [dma((PARTS, 2))])],
                tile_total * 2**22, "local", {6: 2} if last else {7: 3},
            )(
                lists, counts, field, mate, near, *([] if last else [source_factor]),
                pinned(tail), streamed(out),
            )
            source = None if last else source[0]
        near_operands = (lists, counts, pinned(tiles), outer)
        if step == ITERS - 1:
            acc = call(
                last_others_kernel, acc_type, [SMEM, SMEM, VMEM, VMEM, VMEM], VMEM,
                [], tile_total * 2**22, "others", {4: 0},
            )(*near_operands, pinned(acc))
            return call(
                lambda *refs, step=step: last_kernel(step, *refs),
                out_type, [SMEM, SMEM, VMEM, ANY, VMEM, ANY], ANY,
                [picked_type, half_type, done_type, dma((PARTS, 2)), dma((PARTS,))],
                far_flops, "last", {5: 0},
            )(turned_src, far_count, received, target_factor, pinned(acc), streamed(out))
        acc, x = call(
            others_kernel, (acc_type, x_type), [SMEM, SMEM, VMEM, VMEM, VMEM, VMEM], (VMEM, VMEM),
            [], tile_total * 2**22, "others", {5: 0},
        )(*near_operands, pinned(source), pinned(acc))
        width = panels // PARTS * KEPT
        field, send, out, tail = call(
            lambda *refs, step=step: far_kernel(step, *refs),
            (field_type, send_type, out_type, pltpu.VMEM((excite, width), F32)),
            [SMEM, SMEM, SMEM, VMEM, ANY, ANY, VMEM, VMEM, ANY], (VMEM, ANY, ANY, VMEM),
            [
                pltpu.VMEM(gram_shape, BF16), picked_type, picked_type, half_type,
                pltpu.VMEM((excite, panels - width), F32),
                dma((PARTS, 2)), dma((slots,)), dma, dma((PARTS - KEPT,)),
            ],
            far_flops, "far", {8: 2},
        )(
            turned_src, far_count, dest, received, target_factor, streamed(gram), pinned(acc), pinned(x),
            streamed(out),
        )


def solution(mesh):
    in_specs = (
        P(None, "panels"),
        P("panels", None, None, None),
        P("panels", None),
        P("panels"),
        P(),
        P(),
        P(None, None, "panels"),
        P(None, None, "panels"),
    )
    out_specs = P(None, None, "panels")
    return jax.shard_map(shards, mesh=mesh, in_specs=in_specs, out_specs=out_specs, check_vma=False)
```
